128 devices in a mesh: dp: 16 (over y, z), expert: 8 (over x, core).
Axes of the slice: x: 4, y: 4, z: 4, core: 2. Of those that a mesh axis runs over, the one named last changes fastest.
Arguments:
- tokens: bfloat16 [16384, 1440], P(('dp', 'expert')), may hold values from -6 to 6
- out_grad: bfloat16 [16384, 1440], P(('dp', 'expert')), may hold values from -6 to 6
- expert_ids: int32 [16384, 4], P(('dp', 'expert')), may hold values from 0 to 7, all different within a row; in each aligned block of 128 rows (0 to 127, 128 to 255, ...) at most 96 rows name the same one
- probs: bfloat16 [16384, 4], P(('dp', 'expert')), may hold values from 0.099609375 to 0.5
- w_gate: bfloat16 [8, 1440, 1440], P('expert'), may hold values from -0.15625 to 0.15625
- w_up: bfloat16 [8, 1440, 1440], P('expert'), may hold values from -0.15625 to 0.15625
- w_down: bfloat16 [8, 1440, 1440], P('expert'), may hold values from -0.15625 to 0.15625
Outputs:
- grad_tokens: bfloat16 [16384, 1440], P(('dp', 'expert'))
- router_grad: bfloat16 [16384, 4], P(('dp', 'expert'))
- grad_gate: float32 [8, 1440, 1440], P('expert', 'dp')
- grad_up: float32 [8, 1440, 1440], P('expert', 'dp')
- grad_down: float32 [8, 1440, 1440], P('expert', 'dp')
The draws below stay inside these ranges and needn't reach their ends.
Inputs may be any that keep to these rules, and one draw needn't show every extreme that they name: `expert_ids`: each token names 4 different experts; among the tokens of one device no expert is named more than 96 times, a bound that some block reaches.
All inputs are finite; a program needn't handle non-finite values.
Results may differ from the reference program's by a relative error of at most 0.019.
Values may be sent and summed in bfloat16 or wider, within the bound.
A program may use at most 192 MiB of HBM per device.

```python
import math
import jax
import jax.numpy as jnp
import numpy as np
from jax import lax

D = 1440
F = 1440
TOK_DEV = 128
EXPERTS = 8
TOPK = 4
CAP = 96
TOKENS = 16384
N_DP = 16
N_EXPERT = 8


def with_spikes(drawn, key, source, target, blocks, factor):
    owner, partner = [(jnp.arange(drawn.shape[axis_at]) // (drawn.shape[axis_at] // blocks)).reshape([-1 if axis == axis_at else 1 for axis in range(drawn.ndim)]) for axis_at in (source, target)]
    chosen = jax.random.permutation(key, blocks)[partner]
    strong = (owner == chosen) | (owner == (partner + blocks // 2) % blocks)
    return jnp.where(strong, factor * drawn, drawn)


def block_scale(rng, dims, shards, smallest, top_value):
    loudness, own = 1.0, jax.random.fold_in(rng, 6)
    for dim, parts in shards:
        steps = jnp.exp(jax.random.uniform(jax.random.fold_in(own, dim), (parts,), jnp.float32, smallest / len(shards), top_value / len(shards)))
        loudness = loudness * jnp.repeat(steps, dims[dim] // parts).reshape([-1 if axis == dim else 1 for axis in range(len(dims))])
    return loudness


def deal_out(own_key, own, number, rows, number_of, top, limit, slope):
    sequence = jax.random.permutation(own_key, number_of)
    crowded, usual = load_shares(number_of, rows * top, limit, slope, True), load_shares(number_of, rows * top, limit, slope, False)
    places = jnp.arange(number_of)

    def named(lengths, turn):
        used = int((lengths > 0).sum())
        fixed = max(1, used // 4)
        moved = fixed + (places - fixed + turn * (used - fixed)) % max(1, number_of - fixed)
        return jnp.zeros((number_of,), jnp.int32).at[sequence[jnp.where(places < fixed, places, moved)]].set(jnp.asarray(lengths, jnp.int32))

    lengths = jnp.where(number % 4 == 0, named(crowded, number // 4), named(usual, number - number // 4 - 1))
    mixed = jax.random.permutation(jax.random.fold_in(own, 3), number_of)
    donor, taker = mixed[0:number_of // 2 * 2:2], mixed[1:number_of // 2 * 2:2]
    slack = jnp.minimum(lengths[donor] - 1, limit - lengths[taker]) // 2
    slack = jnp.where((donor == sequence[0]) | (taker == sequence[0]) | (lengths[taker] == 0), 0, jnp.maximum(slack, 0))
    moved = jax.random.randint(jax.random.fold_in(own, 4), (number_of // 2,), 0, 1 << 20) % (slack + 1)
    lengths = lengths.at[donor].add(-moved).at[taker].add(moved)
    members = jnp.searchsorted(jnp.cumsum(lengths), jnp.arange(rows * top), side="right").astype(jnp.int32)
    table = members.reshape(top, rows).T
    table = table[jax.random.permutation(jax.random.fold_in(own, 1), rows)]
    turn = jax.random.randint(jax.random.fold_in(own, 2), (rows, 1), 0, top)
    return jnp.take_along_axis(table, (jnp.arange(top)[None, :] + turn) % top, axis=1)


def load_shares(number_of, total, limit, lean, full):
    portions = [(1 << 20) // math.isqrt(standing ** lean) + 1 for standing in range(1, number_of + 1)]
    largest = limit if full else min(limit, max(-(-total // number_of), total * portions[0] // sum(portions)))
    least = 1 if total - largest >= number_of - 1 else 0
    holding, rest = [largest] + [least] * (number_of - 1), total - largest - least * (number_of - 1)
    while rest > 0:
        free = [i for i in range(1, number_of) if holding[i] < largest] or [i for i in range(1, number_of) if holding[i] < limit]
        whole, budget = sum([portions[i] for i in free]), rest
        for i in free:
            extra = min(limit - holding[i], max(1, budget * portions[i] // whole), rest)
            holding[i] = holding[i] + extra
            rest = rest - extra
    return np.array(holding)


def normal_values(own_key, shape, scale, bound, split=(), held_as=jnp.bfloat16):
    drawn = jax.random.normal(own_key, shape, jnp.float32) * scale
    if len(split) > 0:
        drawn = block_scale(own_key, shape, split, -0.22, 0.18) * drawn
    return jnp.clip(drawn, min=-bound, max=bound).astype(held_as)


def bell_draw_with(own_key, extent, deviation, most, pieces, heavy, held_as=jnp.bfloat16):
    entries = deviation * jax.random.normal(own_key, extent, jnp.float32)
    if pieces:
        entries = entries * block_scale(own_key, extent, pieces, -0.22, 0.18)
    return jnp.clip(with_spikes(entries, jax.random.fold_in(own_key, 3), *heavy), -most, most).astype(held_as)


def setup_inputs(seed: int = 0) -> dict:
    arg_keys = jax.random.split(jax.random.key(seed), 8)
    tokens = bell_draw_with(arg_keys[0], (TOKENS, D), 1.0, 6.0, ((0, 128),), (0, 1, 32, 2.75))
    out_grad = normal_values(arg_keys[1], (TOKENS, D), 1.0, 6.0, ((0, 128),))
    expert_ids_keys = jax.random.split(jax.random.fold_in(arg_keys[2], 1), TOKENS // TOK_DEV)
    expert_ids_turns = jax.random.permutation(jax.random.fold_in(arg_keys[2], 3), TOKENS // TOK_DEV)
    expert_ids = jax.vmap(lambda own, number: deal_out(jax.random.fold_in(arg_keys[2], 2), own, number, TOK_DEV, EXPERTS, TOPK, CAP, 1))(expert_ids_keys, expert_ids_turns).reshape((TOKENS, TOPK))
    probs = jnp.clip(0.099609375 + 0.40039062 * jax.random.uniform(arg_keys[3], (TOKENS, TOPK), jnp.float32) ** block_scale(arg_keys[3], (TOKENS, TOPK), ((0, 128),), -0.2, 0.2), 0.099609375, 0.5).astype(jnp.bfloat16)
    w_gate = normal_values(arg_keys[4], (EXPERTS, D, F), D ** -0.5, 0.15625, ((0, 8),))
    w_up = normal_values(arg_keys[5], (EXPERTS, D, F), D ** -0.5, 0.15625, ((0, 8),))
    w_down = normal_values(arg_keys[6], (EXPERTS, F, D), F ** -0.5, 0.15625, ((0, 8),))
    return dict(tokens=tokens, out_grad=out_grad, expert_ids=expert_ids, probs=probs, w_gate=w_gate, w_up=w_up, w_down=w_down)


def expert_pass(inputs, grads, gates, w_gate, w_up, w_down):
    gate_pre = jnp.dot(inputs, w_gate, preferred_element_type=jnp.float32)
    up_pre = jnp.dot(inputs, w_up, preferred_element_type=jnp.float32)
    sigmoid_gate = jax.nn.sigmoid(gate_pre)
    hidden = (gate_pre * sigmoid_gate * up_pre).astype(jnp.bfloat16)
    output = jnp.dot(hidden, w_down, preferred_element_type=jnp.float32)
    prob_grad = jnp.sum(output * grads.astype(jnp.float32), axis=1).astype(jnp.bfloat16)
    out_scaled = (gates.astype(jnp.float32)[:, None] * grads.astype(jnp.float32)).astype(jnp.bfloat16)
    act_grad = lax.dot_general(out_scaled, w_down, (((1,), (1,)), ((), ())), preferred_element_type=jnp.float32)
    gate_grad = (act_grad * up_pre * sigmoid_gate * (1.0 + gate_pre * (1.0 - sigmoid_gate))).astype(jnp.bfloat16)
    up_grad = (act_grad * gate_pre * sigmoid_gate).astype(jnp.bfloat16)
    input_grad = lax.dot_general(gate_grad, w_gate, (((1,), (1,)), ((), ())), preferred_element_type=jnp.float32)
    input_grad = input_grad + lax.dot_general(up_grad, w_up, (((1,), (1,)), ((), ())), preferred_element_type=jnp.float32)
    return input_grad.astype(jnp.bfloat16), prob_grad, hidden, out_scaled, gate_grad, up_grad


def weight_terms(inputs, hidden, out_scaled, gate_grad, up_grad):
    contract = (((0,), (0,)), ((), ()))
    grad_gate = lax.dot_general(inputs, gate_grad, contract, preferred_element_type=jnp.float32)
    grad_up = lax.dot_general(inputs, up_grad, contract, preferred_element_type=jnp.float32)
    grad_down = lax.dot_general(hidden, out_scaled, contract, preferred_element_type=jnp.float32)
    return grad_gate, grad_up, grad_down


def reference(tokens, out_grad, expert_ids, probs, w_gate, w_up, w_down):
    flat_count = TOKENS * TOPK
    expert_slots = N_DP * N_EXPERT * CAP
    flat_ids = expert_ids.reshape(-1)
    flat_probs = probs.reshape(-1)

    def per_expert(expert):
        chosen = flat_ids == expert
        position = jnp.cumsum(chosen.astype(jnp.int32), dtype=jnp.int32) - 1
        target = jnp.where(chosen, position, expert_slots).astype(jnp.int32)
        slot_table = jnp.full((expert_slots,), flat_count, jnp.int32).at[target].set(
            jnp.arange(flat_count, dtype=jnp.int32), mode="drop")
        filled = slot_table < flat_count
        clamped = jnp.minimum(slot_table, flat_count - 1)
        row_index = clamped // TOPK
        inputs = jnp.where(filled[:, None], tokens[row_index], jnp.zeros((), tokens.dtype))
        grads = jnp.where(filled[:, None], out_grad[row_index], jnp.zeros((), out_grad.dtype))
        gates = jnp.where(filled, flat_probs[clamped], jnp.zeros((), probs.dtype))
        input_grad, prob_grad, hidden, out_scaled, gate_grad, up_grad = expert_pass(
            inputs, grads, gates, w_gate[expert], w_up[expert], w_down[expert])
        grad_gate, grad_up, grad_down = weight_terms(inputs, hidden, out_scaled, gate_grad, up_grad)
        return slot_table, input_grad, prob_grad, grad_gate, grad_up, grad_down

    tables, input_grads, prob_grads, grad_gate, grad_up, grad_down = lax.map(
        per_expert, jnp.arange(EXPERTS, dtype=jnp.int32))
    flat_tables = tables.reshape(-1)
    pair_rows = jnp.zeros((flat_count, D), input_grads.dtype).at[flat_tables].set(
        input_grads.reshape(-1, D), mode="drop")
    grad_tokens = jnp.sum(pair_rows.reshape(TOKENS, TOPK, D).astype(jnp.float32), axis=1).astype(jnp.bfloat16)
    router_grad = jnp.zeros((flat_count,), prob_grads.dtype).at[flat_tables].set(
        prob_grads.reshape(-1), mode="drop").reshape(TOKENS, TOPK)
    return grad_tokens, router_grad, grad_gate, grad_up, grad_down
```

```python
import jax
import jax.numpy as jnp
from jax import lax
from jax.sharding import PartitionSpec as P

BF16, F32 = jnp.bfloat16, jnp.float32


def on_device(tokens, out_grad, expert_ids, probs, w_gate, w_up, w_down):
    experts = lax.axis_size("expert")
    groups = lax.axis_size("dp")
    rows, d = tokens.shape
    f = w_gate.shape[2]
    pad = (-d - experts) % 128
    me = lax.axis_index("expert")
    every = jnp.arange(experts, dtype=jnp.int32)
    chosen = expert_ids[:, :, None] == every[None, None, :]
    dense = jnp.sum(jnp.where(chosen, probs[:, :, None].astype(F32), 0.0), axis=1)
    aug = jnp.concatenate(
        [out_grad, dense.astype(BF16), jnp.zeros((rows, pad), BF16)], axis=1
    )
    x = lax.all_gather(tokens, "expert", axis=0, tiled=True)
    both = lax.all_gather(aug, "expert", axis=0, tiled=True)
    og = both[:, :d]
    gate = jnp.sum(
        jnp.where(every[None, :] == me, both[:, d : d + experts].astype(F32), 0.0),
        axis=1,
        keepdims=True,
    )
    g = jnp.dot(x, w_gate[0], preferred_element_type=F32)
    u = jnp.dot(x, w_up[0], preferred_element_type=F32)
    s = jax.nn.sigmoid(g)
    h = g * s * u
    a = lax.dot_general(og, w_down[0], (((1,), (1,)), ((), ())), preferred_element_type=F32)
    r = jnp.sum(h * a, axis=1, keepdims=True)
    pa = gate * a
    gg = (pa * u * s * (1.0 + g * (1.0 - s))).astype(BF16)
    ug = (pa * g * s).astype(BF16)
    hp = (gate * h).astype(BF16)
    contract = (((0,), (0,)), ((), ()))
    terms = [
        lax.dot_general(l, q, contract, preferred_element_type=F32)
        .astype(BF16)
        .reshape(groups, d // groups, f)
        for l, q in ((hp, og), (x, gg), (x, ug))
    ]
    down, gatew, up = [
        lax.psum_scatter(t, "dp", scatter_dimension=0, tiled=False).astype(F32) for t in terms
    ]
    back = (((1,), (1,)), ((), ()))
    ig = lax.dot_general(gg, w_gate[0], back, preferred_element_type=F32)
    ig = ig + lax.dot_general(ug, w_up[0], back, preferred_element_type=F32)
    cols = jnp.where(every[None, :] == me, r, 0.0)
    out = jnp.concatenate([ig, cols, jnp.zeros((ig.shape[0], pad), F32)], axis=1).astype(BF16)
    out = lax.psum_scatter(out, "expert", scatter_dimension=0, tiled=True)
    grad_tokens = out[:, :d]
    router = jnp.sum(
        jnp.where(chosen, out[:, None, d : d + experts].astype(F32), 0.0), axis=2
    ).astype(BF16)
    return grad_tokens, router, gatew[None], up[None], down[None]


def solution(mesh):
    tok = P(("dp", "expert"), None)
    w = P("expert", None, None)
    return jax.shard_map(
        on_device,
        mesh=mesh,
        in_specs=(tok, tok, tok, tok, w, w, w),
        out_specs=(tok, tok, P("expert", "dp", None), P("expert", "dp", None), P("expert", "dp", None)),
        check_vma=False,
    )
```

```python
import functools

import jax
import jax.numpy as jnp
from jax import lax
from jax.experimental import pallas as pl
from jax.experimental.pallas import tpu as pltpu
from jax.sharding import PartitionSpec as P

BF16, F32 = jnp.bfloat16, jnp.float32
MESH = pl.DeviceIdType.MESH
NT = (((1,), (1,)), ((), ()))
NN = (((1,), (0,)), ((), ()))


def mod4(v):
    return lax.rem(v + 8, 4)


def place():
    dp = lax.axis_index("dp")
    ex = lax.axis_index("expert")
    return dp // 4, lax.rem(dp, 4), ex // 2, lax.rem(ex, 2)


def back_kernel(
    xp_h, hp_h, og_h, gg_h, ug_h, wg_h, wu_h, r_h,
    out, ig_out,
    xp, hp, og, gg, ug, wg, wu, terms, r1, r2, ig, sib, rx,
    load, s_send, s_recv, b_send, b_recv, x_send, x_recv,
):
    y, z, x, c = place()
    dp, ex = y * 4 + z, x * 2 + c

    def at(dp_to=None, ex_to=None):
        return (dp if dp_to is None else dp_to, ex if ex_to is None else ex_to)

    def along(axis, d):
        if axis == "y":
            return at(dp_to=mod4(y + d) * 4 + z)
        if axis == "z":
            return at(dp_to=y * 4 + mod4(z + d))
        return at(ex_to=mod4(x + d) * 2 + c)

    loads = [
        pltpu.make_async_copy(a, b, load.at[i])
        for i, (a, b) in enumerate(
            ((hp_h, hp), (og_h, og), (xp_h, xp), (gg_h, gg), (ug_h, ug), (wg_h, wg), (wu_h, wu))
        )
    ]
    for copy in loads:
        copy.start()
    sibling = at(ex_to=x * 2 + 1 - c)
    barrier = pltpu.get_barrier_semaphore()
    for to in [along(a, d) for a in "yzx" for d in (1, -1)] + [sibling]:
        pl.semaphore_signal(barrier, inc=1, device_id=to, device_id_type=MESH)
    pl.semaphore_wait(barrier, 7)

    streams = [("y", 1), ("y", -1), ("z", 1), ("z", -1)]

    def term_at(m, s, index):
        axis, _ = streams[s]
        col = s % 2
        if axis == "y":
            return terms.at[m, col, index, :, 0:48, :]
        return terms.at[m, col, :, index, 48:96, :]

    def first_copy(m, s, t):
        axis, d = streams[s]
        pos = y if axis == "y" else z
        src = term_at(m, s, mod4(pos - d)) if t == 0 else r1.at[m, s, t - 1]
        return pltpu.make_async_remote_copy(
            src_ref=src, dst_ref=r1.at[m, s, t], send_sem=s_send.at[m, s, t],
            recv_sem=s_recv.at[m, s, t], device_id=along(axis, d), device_id_type=MESH,
        )

    def second_copy(m, s, t):
        axis, d = streams[s]
        other = "z" if axis == "y" else "y"
        pos = z if axis == "y" else y
        src = r1.at[m, s, 2, mod4(pos - d)] if t == 0 else r2.at[m, s, t - 1]
        return pltpu.make_async_remote_copy(
            src_ref=src, dst_ref=r2.at[m, s, t], send_sem=s_send.at[m, s, 3 + t],
            recv_sem=s_recv.at[m, s, 3 + t], device_id=along(other, d), device_id_type=MESH,
        )

    def advance(m, stage):
        for s in range(4):
            axis, d = streams[s]
            col = s % 2
            if stage < 3:
                pos = y if axis == "y" else z
                first_copy(m, s, stage).wait_recv()
                index = mod4(pos - d * (2 + stage))

                def add(k, carry, m=m, s=s, axis=axis, index=index, col=col):
                    if axis == "y":
                        own = terms[m, col, index, k, 0:48, :]
                    else:
                        own = terms[m, col, k, index, 48:96, :]
                    r1[m, s, stage, k] = r1[m, s, stage, k] + own
                    return carry

                lax.fori_loop(0, 4, add, 0)
                if stage < 2:
                    first_copy(m, s, stage + 1).start()
                else:
                    second_copy(m, s, 0).start()
            else:
                t = stage - 3
                pos = z if axis == "y" else y
                second_copy(m, s, t).wait_recv()
                own = r1[m, s, 2, mod4(pos - d * (2 + t))]
                if t < 2:
                    r2[m, s, t] = r2[m, s, t] + own
                    second_copy(m, s, t + 1).start()
                else:
                    rows = slice(0, 48) if axis == "y" else slice(48, 96)
                    total = r2[m, s, t].astype(F32) + own.astype(F32)
                    out[m, rows, col * 768 : (col + 1) * 768] = total

    def term(m, lhs, rhs):
        for col, width in ((0, 768), (1, 672)):

            def body(k, carry, col=col, width=width):
                a = lhs[pl.ds(pl.multiple_of(k * 384, 128), 384), :]
                b = rhs[col * 768 : col * 768 + width, :]
                t = lax.dot_general(a, b, NT, preferred_element_type=F32)
                terms[m, col, k, :, :, 0:width] = t.astype(BF16).reshape(4, 96, width)
                return carry

            lax.fori_loop(0, 4, body, 0)
        for s in range(4):
            first_copy(m, s, 0).start()

    def ig_tile(k):
        rows = slice(k * 288, (k + 1) * 288)
        t = lax.dot_general(wg[rows, :], gg[...], NN, preferred_element_type=F32)
        t = t + lax.dot_general(wu[rows, :], ug[...], NN, preferred_element_type=F32)
        t = t.astype(BF16)
        for b in range(8):
            ig[b // 2, b % 2, rows, :] = t[:, b * 128 : (b + 1) * 128]

    sib_copy = pltpu.make_async_remote_copy(
        src_ref=ig.at[:, 1 - c], dst_ref=sib, send_sem=b_send, recv_sem=b_recv,
        device_id=sibling, device_id_type=MESH,
    )
    halves = ((1, 0, 720), (-1, 720, 736))

    def x_copy(h, t):
        d, lo, n = halves[h]
        src = sib.at[mod4(x - d), lo : lo + n] if t == 0 else rx.at[h, t - 1, 0:n]
        return pltpu.make_async_remote_copy(
            src_ref=src, dst_ref=rx.at[h, t, 0:n], send_sem=x_send.at[h, t],
            recv_sem=x_recv.at[h, t], device_id=along("x", d), device_id_type=MESH,
        )

    def ig_pair():
        sib_copy.wait_recv()
        for k in range(4):
            sib[k] = sib[k] + ig[k, c]
        for h in range(2):
            x_copy(h, 0).start()

    def ig_step(t):
        for h in range(2):
            d, lo, n = halves[h]
            x_copy(h, t).wait_recv()
            own = sib[mod4(x - d * (2 + t)), lo : lo + n]
            if t < 2:
                rx[h, t, 0:n] = rx[h, t, 0:n] + own
                x_copy(h, t + 1).start()
            else:
                ig_out[lo : lo + n, :] = (rx[h, t, 0:n].astype(F32) + own.astype(F32)).astype(BF16)

    rowid = lax.broadcasted_iota(jnp.int32, (16, 128), 0)
    for b in range(8):
        row = jnp.broadcast_to(r_h[:, b * 128 : (b + 1) * 128], (16, 128))
        ig[b // 2, b % 2, 1440:1456, :] = jnp.where(rowid == ex, row, 0.0).astype(BF16)

    loads[0].wait()
    loads[1].wait()
    term(0, hp, og)
    loads[2].wait()
    loads[3].wait()
    term(1, xp, gg)
    advance(0, 0)
    loads[4].wait()
    term(2, xp, ug)
    loads[5].wait()
    loads[6].wait()
    advance(1, 0)
    advance(0, 1)
    ig_tile(0)
    advance(2, 0)
    ig_tile(1)
    advance(1, 1)
    ig_tile(2)
    advance(0, 2)
    ig_tile(3)
    advance(2, 1)
    ig_tile(4)
    sib_copy.start()
    advance(1, 2)
    advance(0, 3)
    ig_pair()
    advance(2, 2)
    ig_step(0)
    advance(0, 4)
    advance(1, 3)
    ig_step(1)
    advance(0, 5)
    advance(1, 4)
    advance(2, 3)
    ig_step(2)
    advance(1, 5)
    advance(2, 4)
    advance(2, 5)
    sib_copy.wait_send()
    for h in range(2):
        for t in range(3):
            x_copy(h, t).wait_send()
    for m in range(3):
        for s in range(4):
            for t in range(3):
                first_copy(m, s, t).wait_send()
                second_copy(m, s, t).wait_send()


def back(xp, hp, og, gg, ug, wg, wu, r):
    hbm = pl.BlockSpec(memory_space=pl.ANY)
    vmem = pl.BlockSpec(memory_space=pltpu.VMEM)
    return pl.pallas_call(
        back_kernel,
        out_shape=(
            jax.ShapeDtypeStruct((3, 96, 1536), F32),
            jax.ShapeDtypeStruct((1456, 128), BF16),
        ),
        in_specs=[hbm] * 7 + [vmem],
        out_specs=(vmem, vmem),
        scratch_shapes=[
            pltpu.VMEM(a.shape, BF16) for a in (xp, hp, og, gg, ug, wg, wu)
        ]
        + [
            pltpu.VMEM((3, 2, 4, 4, 96, 768), BF16),
            pltpu.VMEM((3, 4, 3, 4, 48, 768), BF16),
            pltpu.VMEM((3, 4, 3, 48, 768), BF16),
            pltpu.VMEM((4, 2, 1456, 128), BF16),
            pltpu.VMEM((4, 1456, 128), BF16),
            pltpu.VMEM((2, 3, 736, 128), BF16),
            pltpu.SemaphoreType.DMA((7,)),
            pltpu.SemaphoreType.DMA((3, 4, 6)),
            pltpu.SemaphoreType.DMA((3, 4, 6)),
            pltpu.SemaphoreType.DMA,
            pltpu.SemaphoreType.DMA,
            pltpu.SemaphoreType.DMA((2, 3)),
            pltpu.SemaphoreType.DMA((2, 3)),
        ],
        compiler_params=pltpu.CompilerParams(
            collective_id=0, has_side_effects=True, vmem_limit_bytes=64 * 1024 * 1024
        ),
    )(xp, hp, og, gg, ug, wg, wu, r)


def on_device(tokens, out_grad, expert_ids, probs, w_gate, w_up, w_down):
    experts = lax.axis_size("expert")
    groups = lax.axis_size("dp")
    rows, d = tokens.shape
    f = w_gate.shape[2]
    pad = (-d - experts) % 128
    me = lax.axis_index("expert")
    every = jnp.arange(experts, dtype=jnp.int32)
    chosen = expert_ids[:, :, None] == every[None, None, :]
    dense = jnp.sum(jnp.where(chosen, probs[:, :, None].astype(F32), 0.0), axis=1)
    aug = jnp.concatenate(
        [out_grad, dense.astype(BF16), jnp.zeros((rows, pad), BF16)], axis=1
    )
    x = lax.all_gather(tokens, "expert", axis=0, tiled=True)
    both = lax.all_gather(aug, "expert", axis=0, tiled=True)
    og = both[:, :d]
    gate = jnp.sum(
        jnp.where(every[None, :] == me, both[:, d : d + experts].astype(F32), 0.0),
        axis=1,
        keepdims=True,
    )
    g = jnp.dot(x, w_gate[0], preferred_element_type=F32)
    u = jnp.dot(x, w_up[0], preferred_element_type=F32)
    s = jax.nn.sigmoid(g)
    h = g * s * u
    a = lax.dot_general(og, w_down[0], NT, preferred_element_type=F32)
    r = jnp.sum(h * a, axis=1)[None, :]
    pa = gate * a
    gg = (pa * u * s * (1.0 + g * (1.0 - s))).astype(BF16)
    ug = (pa * g * s).astype(BF16)
    hp = (gate * h).astype(BF16)

    def padded(v):
        v = v.T.reshape(groups, d // groups, v.shape[0])
        return jnp.pad(v, ((0, 0), (0, 6), (0, 0))).reshape(-1, v.shape[2])

    out, ig = back(padded(x), padded(hp), og.T, gg.T, ug.T, w_gate[0], w_up[0], r)
    grad_tokens = ig[:d].T
    routed = ig[d : d + experts].T
    router = jnp.sum(jnp.where(chosen, routed[:, None, :].astype(F32), 0.0), axis=2).astype(BF16)
    out = out[:, : d // groups, :f]
    return grad_tokens, router, out[1][None], out[2][None], out[0][None]


def solution(mesh):
    tok = P(("dp", "expert"), None)
    w = P("expert", None, None)
    g = P("expert", "dp", None)
    return jax.shard_map(
        on_device,
        mesh=mesh,
        in_specs=(tok, tok, tok, tok, w, w, w),
        out_specs=(tok, tok, g, g, g),
        check_vma=False,
    )
```

```python
import functools

import jax
import jax.numpy as jnp
from jax import lax
from jax.experimental import pallas as pl
from jax.experimental.pallas import tpu as pltpu
from jax.sharding import PartitionSpec as P

BF16, F32 = jnp.bfloat16, jnp.float32
MESH = pl.DeviceIdType.MESH
NT = (((1,), (1,)), ((), ()))
NN = (((1,), (0,)), ((), ()))
CHIP = 256


def mod4(v):
    return lax.rem(v + 8, 4)


def place():
    dp = lax.axis_index("dp")
    ex = lax.axis_index("expert")
    return dp // 4, lax.rem(dp, 4), ex // 2, lax.rem(ex, 2)


def kernel(
    x_h, og_h, ids, probs, wg_h, wu_h, wd_h,
    out, ig_out, routed,
    xg, og, xp, hp, gg, ug, wa, wb, terms, r1, r2, sib, rx, act, hid, spread, racc,
    load, g_send, g_recv, s_send, s_recv, b_send, b_recv, x_send, x_recv,
):
    y, z, x, c = place()
    dp, ex = y * 4 + z, x * 2 + c

    def at(dp_to=None, ex_to=None):
        return (dp if dp_to is None else dp_to, ex if ex_to is None else ex_to)

    def along(axis, d):
        if axis == "y":
            return at(dp_to=mod4(y + d) * 4 + z)
        if axis == "z":
            return at(dp_to=y * 4 + mod4(z + d))
        return at(ex_to=mod4(x + d) * 2 + c)


    own_x = pltpu.make_async_copy(x_h, xg.at[x, c, 0:1440], load.at[0])
    own_og = pltpu.make_async_copy(og_h, og.at[x, c], load.at[1])
    load_g = pltpu.make_async_copy(wg_h, wa, load.at[2])
    load_u = pltpu.make_async_copy(wu_h, wb, load.at[3])
    load_d = pltpu.make_async_copy(wd_h, wa, load.at[4])
    load_g2 = pltpu.make_async_copy(wg_h, wa, load.at[5])
    for copy in (own_x, own_og, load_g, load_u):
        copy.start()
    sibling = at(ex_to=x * 2 + 1 - c)
    barrier = pltpu.get_barrier_semaphore()
    for to in [along(a, d) for a in "xyz" for d in (1, -1)] + [sibling]:
        pl.semaphore_signal(barrier, inc=1, device_id=to, device_id_type=MESH)

    left, right, far = mod4(x - 1), mod4(x + 1), mod4(x + 2)
    lo, hi = slice(0, 720), slice(720, 1440)

    def hop(a, kind, got=False):
        buf = (xg, og)[a]
        end = slice(720, 1456) if a == 0 else hi
        whole = slice(0, 1456) if a == 0 else slice(0, 1440)
        n, sent, arrived, rows, to = {
            "right": (0, x, left, whole, along("x", 1)),
            "left": (1, x, right, whole, along("x", -1)),
            "pass_right": (2, left, far, lo, along("x", 1)),
            "pass_left": (3, right, far, end, along("x", -1)),
            "core_own": (4, x, x, whole, sibling),
            "core_left": (5, left, left, whole, sibling),
            "core_right": (6, right, right, whole, sibling),
            "core_far": (7, far, far, whole, sibling),
        }[kind]
        core = 1 - c if got and n >= 4 else c
        block = buf.at[arrived if got else sent, core, rows]
        return pltpu.make_async_remote_copy(
            src_ref=block, dst_ref=block, send_sem=g_send.at[a, n], recv_sem=g_recv.at[a, n],
            device_id=to, device_id_type=MESH,
        )

    kinds = (
        "right", "left", "core_own", "pass_right", "pass_left", "core_left", "core_right", "core_far",
    )

    def send(a, *names):
        for name in names:
            hop(a, name).start()

    def got(a, *names):
        for name in names:
            hop(a, name, got=True).wait_recv()

    rowid = lax.broadcasted_iota(jnp.int32, (16, 128), 0)
    dense = jnp.zeros((16, 128), F32)
    for k in range(4):
        dense = dense + jnp.where(ids[k : k + 1, :] == rowid, probs[k : k + 1, :].astype(F32), 0.0)
    xg[x, c, 1440:1456, :] = dense.astype(BF16)
    pl.semaphore_wait(barrier, 7)
    own_x.wait()
    send(0, "right", "left", "core_own")

    row = lax.broadcasted_iota(jnp.int32, (768, 720), 0)
    col = lax.broadcasted_iota(jnp.int32, (768, 720), 1)
    inside = lax.rem(row, 96)
    picked = (inside < 90) & (lax.div(row, 96) * 90 + inside == col)
    spread[...] = jnp.where(picked, 1.0, 0.0).astype(BF16)

    def flip(w, m):
        for k in range(4):
            n = 384 if k < 3 else 288
            t = w[:, k * 384 : k * 384 + n].T.reshape(n // 96, 96, 1440)
            terms[m, 0, k, 0 : n // 96] = t[:, :, 0:768]
            terms[m, 1, k, 0 : n // 96, :, 0:672] = t[:, :, 768:1440]

    def lanes_of(chip):
        return pl.ds(pl.multiple_of(chip * CHIP, CHIP), CHIP)

    def forward(chip):
        cols = jnp.concatenate([xg[chip, 0, 0:1440, :], xg[chip, 1, 0:1440, :]], axis=1)
        for m, to in ((0, gg), (1, ug)):
            for k in range(4):
                n = 384 if k < 3 else 288
                a = terms[m, 0, k, 0 : n // 96].reshape(n, 768)
                b = terms[m, 1, k, 0 : n // 96, :, 0:672].reshape(n, 672)
                t = lax.dot_general(a, cols[0:768], NN, preferred_element_type=F32)
                t = t + lax.dot_general(b, cols[768:1440], NN, preferred_element_type=F32)
                to[k * 384 : k * 384 + n, lanes_of(chip)] = t.astype(BF16)

    def widen(chip):
        for h in range(2):
            rows = slice(h * 720, h * 720 + 720)
            v = jnp.concatenate([xg[chip, 0, rows, :], xg[chip, 1, rows, :]], axis=1)
            t = lax.dot_general(spread[...], v, NN, preferred_element_type=F32)
            xp[h * 768 : h * 768 + 768, lanes_of(chip)] = t.astype(BF16)

    def gradient(chip):
        lanes = lanes_of(chip)
        gate = jnp.concatenate(
            [
                jnp.sum(
                    jnp.where(rowid == ex, xg[chip, k, 1440:1456, :].astype(F32), 0.0),
                    axis=0,
                    keepdims=True,
                )
                for k in range(2)
            ],
            axis=1,
        )
        cols = jnp.concatenate([og[chip, 0], og[chip, 1]], axis=1)
        total = jnp.zeros((16, CHIP), F32)
        for h in range(2):
            act[...] = lax.dot_general(
                wa[h * 720 : h * 720 + 720, :], cols, NN, preferred_element_type=F32
            )

            def body(i, total, h=h):
                r0 = pl.multiple_of(i * 16, 16)
                rows = pl.ds(pl.multiple_of(h * 720 + i * 16, 16), 16)
                a = act[pl.ds(r0, 16), :]
                g = gg[rows, lanes].astype(F32)
                u = ug[rows, lanes].astype(F32)
                s = jax.nn.sigmoid(g)
                gs = g * s
                hidden = gs * u
                pa = gate * a
                gg[rows, lanes] = (pa * u * s * (1.0 + g * (1.0 - s))).astype(BF16)
                ug[rows, lanes] = (pa * gs).astype(BF16)
                hid[pl.ds(r0, 16), :] = (gate * hidden).astype(BF16)
                return total + hidden * a

            total = lax.fori_loop(0, 45, body, total, unroll=3)
            t = lax.dot_general(spread[...], hid[...], NN, preferred_element_type=F32)
            hp[h * 768 : h * 768 + 768, lanes] = t.astype(BF16)
        racc[:, lanes] = jnp.sum(total, axis=0, keepdims=True)

    streams = [("y", 1), ("y", -1), ("z", 1), ("z", -1)]

    def term_at(m, s, index):
        axis, _ = streams[s]
        col = s % 2
        if axis == "y":
            return terms.at[m, col, index, :, 0:48, :]
        return terms.at[m, col, :, index, 48:96, :]

    def first_copy(m, s, t):
        axis, d = streams[s]
        pos = y if axis == "y" else z
        src = term_at(m, s, mod4(pos - d)) if t == 0 else r1.at[m, s, t - 1]
        return pltpu.make_async_remote_copy(
            src_ref=src, dst_ref=r1.at[m, s, t], send_sem=s_send.at[m, s, t],
            recv_sem=s_recv.at[m, s, t], device_id=along(axis, d), device_id_type=MESH,
        )

    def second_copy(m, s, t):
        axis, d = streams[s]
        other = "z" if axis == "y" else "y"
        pos = z if axis == "y" else y
        src = r1.at[m, s, 2, mod4(pos - d)] if t == 0 else r2.at[m, s, t - 1]
        return pltpu.make_async_remote_copy(
            src_ref=src, dst_ref=r2.at[m, s, t], send_sem=s_send.at[m, s, 3 + t],
            recv_sem=s_recv.at[m, s, 3 + t], device_id=along(other, d), device_id_type=MESH,
        )

    def advance(m, stage):
        for s in range(4):
            axis, d = streams[s]
            col = s % 2
            if stage < 3:
                pos = y if axis == "y" else z
                first_copy(m, s, stage).wait_recv()
                index = mod4(pos - d * (2 + stage))

                def add(k, carry, m=m, s=s, axis=axis, index=index, col=col):
                    if axis == "y":
                        own = terms[m, col, index, k, 0:48, :]
                    else:
                        own = terms[m, col, k, index, 48:96, :]
                    r1[m, s, stage, k] = r1[m, s, stage, k] + own
                    return carry

                lax.fori_loop(0, 4, add, 0)
                if stage < 2:
                    first_copy(m, s, stage + 1).start()
                else:
                    second_copy(m, s, 0).start()
            else:
                t = stage - 3
                pos = z if axis == "y" else y
                second_copy(m, s, t).wait_recv()
                own = r1[m, s, 2, mod4(pos - d * (2 + t))]
                if t < 2:
                    r2[m, s, t] = r2[m, s, t] + own
                    second_copy(m, s, t + 1).start()
                else:
                    rows = slice(0, 48) if axis == "y" else slice(48, 96)
                    total = r2[m, s, t].astype(F32) + own.astype(F32)
                    out[m, rows, col * 768 : (col + 1) * 768] = total

    def term(m, lhs, rhs):
        for col, width in ((0, 768), (1, 672)):

            def body(k, carry, col=col, width=width):
                a = lhs[pl.ds(pl.multiple_of(k * 384, 128), 384), :]
                b = rhs(slice(col * 768, col * 768 + width))
                t = lax.dot_general(a, b, NT, preferred_element_type=F32)
                terms[m, col, k, :, :, 0:width] = t.astype(BF16).reshape(4, 96, width)
                return carry

            lax.fori_loop(0, 4, body, 0)
        for s in range(4):
            first_copy(m, s, 0).start()

    def ig_tile(k):
        rows = slice(k * 288, (k + 1) * 288)
        t = lax.dot_general(wa[rows, :], gg[...], NN, preferred_element_type=F32)
        t = t + lax.dot_general(wb[rows, :], ug[...], NN, preferred_element_type=F32)
        t = t.astype(BF16)
        for b in range(8):
            xg[b // 2, b % 2, rows, :] = t[:, b * 128 : (b + 1) * 128]

    sib_copy = pltpu.make_async_remote_copy(
        src_ref=xg.at[:, 1 - c], dst_ref=sib, send_sem=b_send, recv_sem=b_recv,
        device_id=sibling, device_id_type=MESH,
    )
    halves = ((1, 0, 720), (-1, 720, 736))

    def x_copy(h, t):
        d, lo, n = halves[h]
        src = sib.at[mod4(x - d), lo : lo + n] if t == 0 else rx.at[h, t - 1, 0:n]
        return pltpu.make_async_remote_copy(
            src_ref=src, dst_ref=rx.at[h, t, 0:n], send_sem=x_send.at[h, t],
            recv_sem=x_recv.at[h, t], device_id=along("x", d), device_id_type=MESH,
        )

    def ig_pair():
        sib_copy.wait_recv()
        for k in range(4):
            sib[k] = sib[k] + xg[k, c]
        for h in range(2):
            x_copy(h, 0).start()

    def ig_step(t):
        for h in range(2):
            d, lo, n = halves[h]
            x_copy(h, t).wait_recv()
            own = sib[mod4(x - d * (2 + t)), lo : lo + n]
            if t < 2:
                rx[h, t, 0:n] = rx[h, t, 0:n] + own
                x_copy(h, t + 1).start()
            else:
                total = rx[h, t, 0:n].astype(F32) + own.astype(F32)
                ig_out[lo : lo + 720, :] = total[0:720].astype(BF16)
                if h == 1:
                    for k in range(4):
                        mine = jnp.where(ids[k : k + 1, :] == rowid, total[720:736], 0.0)
                        routed[k : k + 1, :] = jnp.sum(mine, axis=0, keepdims=True).astype(BF16)

    load_g.wait()
    flip(wa, 0)
    load_d.start()
    load_u.wait()
    flip(wb, 1)
    own_og.wait()
    got(0, "right")
    send(0, "pass_right", "core_left")
    got(0, "left")
    send(0, "pass_left", "core_right")
    send(1, "right", "left", "core_own")
    got(0, "core_own")
    forward(x)
    got(0, "core_left")
    forward(left)
    got(0, "core_right")
    forward(right)
    got(0, "pass_right", "pass_left")
    send(0, "core_far")
    widen(x)
    widen(left)
    widen(right)
    got(1, "right")
    send(1, "pass_right", "core_left")
    got(1, "left")
    send(1, "pass_left", "core_right")
    got(0, "core_far")
    forward(far)
    widen(far)
    load_d.wait()
    got(1, "core_own")
    gradient(x)
    got(1, "pass_right", "pass_left")
    send(1, "core_far")
    got(1, "core_left")
    gradient(left)
    got(1, "core_right")
    gradient(right)
    got(1, "core_far")
    gradient(far)
    load_g2.start()

    def og_rows(rows):
        return jnp.concatenate([og[b // 2, b % 2, rows, :] for b in range(8)], axis=1)

    term(0, hp, og_rows)
    term(1, xp, lambda rows: gg[rows, :])
    for name in kinds:
        hop(0, name).wait_send()
    for b in range(8):
        part = jnp.broadcast_to(racc[:, b * 128 : (b + 1) * 128], (16, 128))
        xg[b // 2, b % 2, 1440:1456, :] = jnp.where(rowid == ex, part, 0.0).astype(BF16)
    advance(0, 0)
    term(2, xp, lambda rows: ug[rows, :])
    load_g2.wait()
    advance(1, 0)
    advance(0, 1)
    ig_tile(0)
    advance(2, 0)
    ig_tile(1)
    advance(1, 1)
    ig_tile(2)
    advance(0, 2)
    ig_tile(3)
    advance(2, 1)
    ig_tile(4)
    sib_copy.start()
    advance(1, 2)
    advance(0, 3)
    ig_pair()
    advance(2, 2)
    ig_step(0)
    advance(0, 4)
    advance(1, 3)
    ig_step(1)
    advance(0, 5)
    advance(1, 4)
    advance(2, 3)
    ig_step(2)
    advance(1, 5)
    advance(2, 4)
    advance(2, 5)
    sib_copy.wait_send()
    for h in range(2):
        for t in range(3):
            x_copy(h, t).wait_send()
    for m in range(3):
        for s in range(4):
            for t in range(3):
                first_copy(m, s, t).wait_send()
                second_copy(m, s, t).wait_send()
    for name in kinds:
        hop(1, name).wait_send()


def layer(x, og, ids, probs, wg, wu, wd):
    hbm = pl.BlockSpec(memory_space=pl.ANY)
    vmem = pl.BlockSpec(memory_space=pltpu.VMEM)
    return pl.pallas_call(
        kernel,
        out_shape=(
            jax.ShapeDtypeStruct((3, 96, 1536), F32),
            jax.ShapeDtypeStruct((1440, 128), BF16),
            jax.ShapeDtypeStruct((4, 128), BF16),
        ),
        in_specs=[hbm, hbm, vmem, vmem, hbm, hbm, hbm],
        out_specs=(vmem, vmem, vmem),
        scratch_shapes=[
            pltpu.VMEM((4, 2, 1456, 128), BF16),
            pltpu.VMEM((4, 2, 1440, 128), BF16),
            pltpu.VMEM((1536, 1024), BF16),
            pltpu.VMEM((1536, 1024), BF16),
            pltpu.VMEM((1440, 1024), BF16),
            pltpu.VMEM((1440, 1024), BF16),
            pltpu.VMEM((1440, 1440), BF16),
            pltpu.VMEM((1440, 1440), BF16),
            pltpu.VMEM((3, 2, 4, 4, 96, 768), BF16),
            pltpu.VMEM((3, 4, 3, 4, 48, 768), BF16),
            pltpu.VMEM((3, 4, 3, 48, 768), BF16),
            pltpu.VMEM((4, 1456, 128), BF16),
            pltpu.VMEM((2, 3, 736, 128), BF16),
            pltpu.VMEM((720, CHIP), F32),
            pltpu.VMEM((720, CHIP), BF16),
            pltpu.VMEM((768, 720), BF16),
            pltpu.VMEM((1, 1024), F32),
            pltpu.SemaphoreType.DMA((6,)),
            pltpu.SemaphoreType.DMA((2, 8)),
            pltpu.SemaphoreType.DMA((2, 8)),
            pltpu.SemaphoreType.DMA((3, 4, 6)),
            pltpu.SemaphoreType.DMA((3, 4, 6)),
            pltpu.SemaphoreType.DMA,
            pltpu.SemaphoreType.DMA,
            pltpu.SemaphoreType.DMA((2, 3)),
            pltpu.SemaphoreType.DMA((2, 3)),
        ],
        compiler_params=pltpu.CompilerParams(
            collective_id=0, has_side_effects=True, vmem_limit_bytes=64 * 1024 * 1024
        ),
    )(x, og, ids, probs, wg, wu, wd)


def on_device(tokens, out_grad, expert_ids, probs, w_gate, w_up, w_down):
    out, ig, routed = layer(
        tokens.T, out_grad.T, expert_ids.T, probs.T, w_gate[0], w_up[0], w_down[0]
    )
    out = out[:, :90, :1440]
    return ig.T, routed.T, out[1][None], out[2][None], out[0][None]


def solution(mesh):
    tok = P(("dp", "expert"), None)
    w = P("expert", None, None)
    g = P("expert", "dp", None)
    return jax.shard_map(
        on_device,
        mesh=mesh,
        in_specs=(tok, tok, tok, tok, w, w, w),
        out_specs=(tok, tok, g, g, g),
        check_vma=False,
    )
```

```python
import functools

import jax
import jax.numpy as jnp
from jax import lax
from jax.experimental import pallas as pl
from jax.experimental.pallas import tpu as pltpu
from jax.sharding import PartitionSpec as P

BF16, F32 = jnp.bfloat16, jnp.float32
MESH = pl.DeviceIdType.MESH
NT = (((1,), (1,)), ((), ()))
NN = (((1,), (0,)), ((), ()))
CHIP = 256


def mod4(v):
    return lax.rem(v + 8, 4)


def place():
    dp = lax.axis_index("dp")
    ex = lax.axis_index("expert")
    return dp // 4, lax.rem(dp, 4), ex // 2, lax.rem(ex, 2)


def kernel(
    x_h, og_h, ids, probs, wg_h, wu_h, wd_h,
    out_d, out_g, out_u, ig_out, routed,
    xg, og, xp, hp, gg, ug, wa, wb, wt, first, own, r1, r2, sib, rx, spread, racc,
    load, g_send, g_recv, s_send, s_recv, b_send, b_recv, x_send, x_recv,
):
    y, z, x, c = place()
    dp, ex = y * 4 + z, x * 2 + c

    def at(dp_to=None, ex_to=None):
        return (dp if dp_to is None else dp_to, ex if ex_to is None else ex_to)

    def along(axis, d):
        if axis == "y":
            return at(dp_to=mod4(y + d) * 4 + z)
        if axis == "z":
            return at(dp_to=y * 4 + mod4(z + d))
        return at(ex_to=mod4(x + d) * 2 + c)


    own_x = pltpu.make_async_copy(x_h, xg.at[x, c, 0:1440], load.at[0])
    own_og = pltpu.make_async_copy(og_h, og.at[x, c], load.at[1])
    load_g = pltpu.make_async_copy(wg_h, wa, load.at[2])
    load_u = pltpu.make_async_copy(wu_h, wb, load.at[3])
    load_d = pltpu.make_async_copy(wd_h, wa, load.at[4])
    load_g2 = pltpu.make_async_copy(wg_h, wa, load.at[5])
    for copy in (own_x, own_og, load_g, load_u):
        copy.start()
    sibling = at(ex_to=x * 2 + 1 - c)
    barrier = pltpu.get_barrier_semaphore()
    for to in [along(a, d) for a in "xyz" for d in (1, -1)] + [sibling]:
        pl.semaphore_signal(barrier, inc=1, device_id=to, device_id_type=MESH)

    left, right, far = mod4(x - 1), mod4(x + 1), mod4(x + 2)

    def hop(a, kind, half, got=False):
        buf = (xg, og)[a]
        rows = slice(0, 768) if half == 0 else slice(768, 1456 if a == 0 else 1440)
        n, sent, arrived, to = {
            "right": (0, x, left, along("x", 1)),
            "left": (1, x, right, along("x", -1)),
            "pass_right": (2, left, far, along("x", 1)),
            "pass_left": (3, right, far, along("x", -1)),
            "core_own": (4, x, x, sibling),
            "core_left": (5, left, left, sibling),
            "core_right": (6, right, right, sibling),
            "core_far": (7, far, far, sibling),
        }[kind]
        core = 1 - c if got and n >= 4 else c
        block = buf.at[arrived if got else sent, core, rows]
        return pltpu.make_async_remote_copy(
            src_ref=block, dst_ref=block, send_sem=g_send.at[a, n, half],
            recv_sem=g_recv.at[a, n, half], device_id=to, device_id_type=MESH,
        )

    sent = []

    def send(a, *names):
        for name, half in names:
            hop(a, name, half).start()
            sent.append((a, name, half))

    def got(a, *names):
        for name, half in names:
            hop(a, name, half, got=True).wait_recv()

    def both(name):
        return (name, 0), (name, 1)

    rowid = lax.broadcasted_iota(jnp.int32, (16, 128), 0)
    dense = jnp.zeros((16, 128), F32)
    for k in range(4):
        dense = dense + jnp.where(ids[k : k + 1, :] == rowid, probs[k : k + 1, :].astype(F32), 0.0)
    xg[x, c, 1440:1456, :] = dense.astype(BF16)
    own_x.wait()
    pl.semaphore_wait(barrier, 7)
    send(0, ("right", 0), ("left", 1), *both("core_own"), ("right", 1), ("left", 0))

    row = lax.broadcasted_iota(jnp.int32, (768, 720), 0)
    col = lax.broadcasted_iota(jnp.int32, (768, 720), 1)
    rest = row - 384
    above = lax.div(row, 192) * 360 + lax.div(lax.rem(row, 192), 48) * 90 + lax.rem(row, 48)
    below = lax.rem(lax.div(rest, 48), 2) * 360 + lax.div(rest, 96) * 90 + 48 + lax.rem(rest, 48)
    kept = lax.rem(row, 48) < 42
    picked = ((row < 384) & (above == col)) | ((row >= 384) & kept & (below == col))
    spread[...] = jnp.where(picked, 1.0, 0.0).astype(BF16)

    def flip(w, m):
        for k in range(4):
            n = 384 if k < 3 else 288
            wt[m, k * 384 : k * 384 + n, :] = w[:, k * 384 : k * 384 + n].T

    def lanes_of(chip):
        return pl.ds(pl.multiple_of(chip * CHIP, CHIP), CHIP)

    def gate_of(chip):
        parts = []
        for k in range(2):
            rows = xg[chip, k, 1440:1456, :].astype(F32)
            parts.append(jnp.sum(jnp.where(rowid == ex, rows, 0.0), axis=0, keepdims=True))
        return jnp.concatenate(parts, axis=1)

    def place_rows(to, h, v, lanes):
        t = lax.dot_general(spread[...], v, NN, preferred_element_type=F32).astype(BF16)
        to[h * 384 : h * 384 + 384, lanes] = t[0:384]
        for k in range(4):
            r0 = 768 + k * 192 + h * 96
            to[r0 : r0 + 96, lanes] = t[384 + k * 96 : 480 + k * 96]

    def forward(chip):
        lanes = lanes_of(chip)
        gate = gate_of(chip)
        cols = jnp.concatenate([xg[chip, 0, 0:1440, :], xg[chip, 1, 0:1440, :]], axis=1)
        for h in range(2):
            rows = slice(h * 720, h * 720 + 720)
            g = lax.dot_general(wt[0, rows, :], cols, NN, preferred_element_type=F32)
            u = lax.dot_general(wt[1, rows, :], cols, NN, preferred_element_type=F32)
            s = 0.5 * jnp.tanh(0.5 * g) + 0.5
            gs = g * s
            hidden = gs * u
            gg[rows, lanes] = (u * (s + gs * (1.0 - s))).astype(BF16)
            ug[rows, lanes] = gs.astype(BF16)
            xp[rows, lanes] = hidden.astype(BF16)
            place_rows(hp, h, (gate * hidden).astype(BF16), lanes)

    def gradient(chip):
        lanes = lanes_of(chip)
        gate = gate_of(chip)
        cols = jnp.concatenate([og[chip, 0], og[chip, 1]], axis=1)
        total = jnp.zeros((1, CHIP), F32)
        for h in range(2):
            rows = slice(h * 720, h * 720 + 720)
            a = lax.dot_general(wa[rows, :], cols, NN, preferred_element_type=F32)
            pa = gate * a
            gg[rows, lanes] = (pa * gg[rows, lanes].astype(F32)).astype(BF16)
            ug[rows, lanes] = (pa * ug[rows, lanes].astype(F32)).astype(BF16)
            hidden = xp[rows, lanes].astype(F32)
            total = total + jnp.sum(hidden * a, axis=0, keepdims=True)
        racc[:, lanes] = total

    def widen(chip):
        for h in range(2):
            rows = slice(h * 720, h * 720 + 720)
            v = jnp.concatenate([xg[chip, 0, rows, :], xg[chip, 1, rows, :]], axis=1)
            place_rows(xp, h, v, lanes_of(chip))

    streams = [("y", 1), ("y", -1), ("z", 1), ("z", -1)]
    rings = {"y": y, "z": z}

    def product(m, s, index):
        lhs = hp if m == 0 else xp
        r0 = pl.multiple_of((s // 2) * 768 + index * 192, 64)
        a = lhs[pl.ds(r0, 192), :]
        cols = slice(0, 768) if s % 2 == 0 else slice(768, 1440)
        if m == 0:
            b = jnp.concatenate([og[k // 2, k % 2, cols, :] for k in range(8)], axis=1)
        else:
            b = (gg, ug)[m - 1][cols, :]
        return lax.dot_general(a, b, NT, preferred_element_type=F32)

    def first_copy(m, s, t):
        axis, d = streams[s]
        return pltpu.make_async_remote_copy(
            src_ref=first.at[m, s] if t == 0 else r1.at[m, s, t - 1], dst_ref=r1.at[m, s, t],
            send_sem=s_send.at[m, s, t], recv_sem=s_recv.at[m, s, t],
            device_id=along(axis, d), device_id_type=MESH,
        )

    def share(index):
        return pl.ds(pl.multiple_of(index * 48, 16), 48)

    def second_copy(m, s, t):
        axis, d = streams[s]
        other = "z" if axis == "y" else "y"
        src = r1.at[m, s, 2, share(mod4(rings[other] - d))] if t == 0 else r2.at[m, s, t - 1]
        return pltpu.make_async_remote_copy(
            src_ref=src, dst_ref=r2.at[m, s, t], send_sem=s_send.at[m, s, 3 + t],
            recv_sem=s_recv.at[m, s, 3 + t], device_id=along(other, d), device_id_type=MESH,
        )

    def start(m, *which):
        for s in which:
            axis, d = streams[s]
            t = product(m, s, mod4(rings[axis] - d)).astype(BF16)
            first[m, s, :, 0 : t.shape[1]] = t
            first_copy(m, s, 0).start()

    def advance(m, stage):
        if stage < 3:
            for s in range(4):
                axis, d = streams[s]
                t = product(m, s, mod4(rings[axis] - d * (2 + stage)))
                own[s, :, 0 : t.shape[1]] = t
        for s in range(4):
            axis, d = streams[s]
            if stage < 3:
                first_copy(m, s, stage).wait_recv()

                def add(k, carry, s=s):
                    rows = share(k)
                    t = r1[m, s, stage, rows, :].astype(F32) + own[s, rows, :]
                    r1[m, s, stage, rows, :] = t.astype(BF16)
                    return carry

                lax.fori_loop(0, 4, add, 0)
                if stage < 2:
                    first_copy(m, s, stage + 1).start()
                else:
                    second_copy(m, s, 0).start()
            else:
                t = stage - 3
                other = "z" if axis == "y" else "y"
                second_copy(m, s, t).wait_recv()
                mine = r1[m, s, 2, share(mod4(rings[other] - d * (2 + t))), :].astype(F32)
                total = r2[m, s, t].astype(F32) + mine
                if t < 2:
                    r2[m, s, t] = total.astype(BF16)
                    second_copy(m, s, t + 1).start()
                else:
                    n = 48 if axis == "y" else 42
                    r0 = 0 if axis == "y" else 48
                    to = (out_d, out_g, out_u)[m]
                    if s % 2 == 0:
                        to[r0 : r0 + n, 0:768] = total[0:n]
                    else:
                        to[r0 : r0 + n, 768:1440] = total[0:n, 0:672]

    def ig_tile(k):
        rows = slice(k * 288, (k + 1) * 288)
        t = lax.dot_general(wa[rows, :], gg[...], NN, preferred_element_type=F32)
        t = t + lax.dot_general(wb[rows, :], ug[...], NN, preferred_element_type=F32)
        t = t.astype(BF16)
        for b in range(8):
            xg[b // 2, b % 2, rows, :] = t[:, b * 128 : (b + 1) * 128]

    sib_copy = pltpu.make_async_remote_copy(
        src_ref=xg.at[:, 1 - c], dst_ref=sib, send_sem=b_send, recv_sem=b_recv,
        device_id=sibling, device_id_type=MESH,
    )
    halves = ((1, 0, 720), (-1, 720, 736))

    def x_copy(h, t):
        d, lo, n = halves[h]
        src = sib.at[mod4(x - d), lo : lo + n] if t == 0 else rx.at[h, t - 1, 0:n]
        return pltpu.make_async_remote_copy(
            src_ref=src, dst_ref=rx.at[h, t, 0:n], send_sem=x_send.at[h, t],
            recv_sem=x_recv.at[h, t], device_id=along("x", d), device_id_type=MESH,
        )

    def ig_pair():
        sib_copy.wait_recv()
        for k in range(4):
            sib[k] = sib[k] + xg[k, c]
        for h in range(2):
            x_copy(h, 0).start()

    def ig_step(t):
        for h in range(2):
            d, lo, n = halves[h]
            x_copy(h, t).wait_recv()
            own = sib[mod4(x - d * (2 + t)), lo : lo + n]
            if t < 2:
                rx[h, t, 0:n] = rx[h, t, 0:n] + own
                x_copy(h, t + 1).start()
            else:
                total = rx[h, t, 0:n].astype(F32) + own.astype(F32)
                ig_out[lo : lo + 720, :] = total[0:720].astype(BF16)
                if h == 1:
                    for k in range(4):
                        mine = jnp.where(ids[k : k + 1, :] == rowid, total[720:736], 0.0)
                        routed[k : k + 1, :] = jnp.sum(mine, axis=0, keepdims=True).astype(BF16)

    load_g.wait()
    flip(wa, 0)
    load_d.start()
    load_u.wait()
    flip(wb, 1)
    got(0, ("right", 0))
    send(0, ("pass_right", 0))
    got(0, ("left", 1))
    send(0, ("pass_left", 1))
    own_og.wait()
    send(1, ("right", 0), ("left", 0), ("core_own", 0), ("right", 1), ("left", 1), ("core_own", 1))
    got(0, *both("core_own"))
    forward(x)
    got(0, ("right", 1))
    send(0, *both("core_left"))
    got(0, ("left", 0))
    send(0, *both("core_right"))
    got(0, *both("core_left"))
    forward(left)
    got(0, ("pass_right", 0), ("pass_left", 1))
    send(0, *both("core_far"))
    got(0, *both("core_right"))
    forward(right)
    got(1, ("right", 0))
    send(1, ("pass_right", 0), ("core_left", 0))
    got(1, ("left", 0))
    send(1, ("core_right", 0))
    got(0, *both("core_far"))
    forward(far)
    got(1, ("left", 1))
    send(1, ("pass_left", 1), ("core_right", 1))
    got(1, ("right", 1))
    send(1, ("core_left", 1))
    got(1, ("pass_right", 0))
    send(1, ("core_far", 0))
    got(1, ("core_own", 0), ("core_left", 0), ("core_right", 0), ("core_far", 0))
    start(0, 0, 2)
    load_d.wait()
    got(1, ("core_own", 1))
    gradient(x)
    got(1, ("pass_left", 1))
    send(1, ("core_far", 1))
    got(1, ("core_left", 1), ("core_right", 1), ("core_far", 1))
    start(0, 1, 3)
    gradient(left)
    gradient(right)
    advance(0, 0)
    gradient(far)
    load_g2.start()
    for chip in range(4):
        widen(chip)
    start(1, 0, 1, 2, 3)
    for a, name, half in sent:
        if a == 0:
            hop(a, name, half).wait_send()
    for b in range(8):
        part = jnp.broadcast_to(racc[:, b * 128 : (b + 1) * 128], (16, 128))
        xg[b // 2, b % 2, 1440:1456, :] = jnp.where(rowid == ex, part, 0.0).astype(BF16)
    advance(0, 1)
    start(2, 0, 1, 2, 3)
    load_g2.wait()
    advance(1, 0)
    ig_tile(0)
    advance(0, 2)
    ig_tile(1)
    advance(2, 0)
    ig_tile(2)
    advance(1, 1)
    ig_tile(3)
    advance(2, 1)
    ig_tile(4)
    sib_copy.start()
    advance(0, 3)
    advance(1, 2)
    ig_pair()
    advance(0, 4)
    advance(2, 2)
    ig_step(0)
    advance(0, 5)
    advance(1, 3)
    ig_step(1)
    advance(1, 4)
    advance(2, 3)
    ig_step(2)
    advance(1, 5)
    advance(2, 4)
    advance(2, 5)
    sib_copy.wait_send()
    for h in range(2):
        for t in range(3):
            x_copy(h, t).wait_send()
    for m in range(3):
        for s in range(4):
            for t in range(3):
                first_copy(m, s, t).wait_send()
                second_copy(m, s, t).wait_send()
    for a, name, half in sent:
        if a == 1:
            hop(a, name, half).wait_send()


def layer(x, og, ids, probs, wg, wu, wd):
    hbm = pl.BlockSpec(memory_space=pl.ANY)
    vmem = pl.BlockSpec(memory_space=pltpu.VMEM)
    return pl.pallas_call(
        kernel,
        out_shape=(
            jax.ShapeDtypeStruct((90, 1440), F32),
            jax.ShapeDtypeStruct((90, 1440), F32),
            jax.ShapeDtypeStruct((90, 1440), F32),
            jax.ShapeDtypeStruct((1440, 128), BF16),
            jax.ShapeDtypeStruct((4, 128), BF16),
        ),
        in_specs=[hbm, hbm, vmem, vmem, hbm, hbm, hbm],
        out_specs=(vmem,) * 5,
        scratch_shapes=[
            pltpu.VMEM((4, 2, 1456, 128), BF16),
            pltpu.VMEM((4, 2, 1440, 128), BF16),
            pltpu.VMEM((1536, 1024), BF16),
            pltpu.VMEM((1536, 1024), BF16),
            pltpu.VMEM((1440, 1024), BF16),
            pltpu.VMEM((1440, 1024), BF16),
            pltpu.VMEM((1440, 1440), BF16),
            pltpu.VMEM((1440, 1440), BF16),
            pltpu.VMEM((2, 1440, 1440), BF16),
            pltpu.VMEM((3, 4, 192, 768), BF16),
            pltpu.VMEM((4, 192, 768), F32),
            pltpu.VMEM((3, 4, 3, 192, 768), BF16),
            pltpu.VMEM((3, 4, 3, 48, 768), BF16),
            pltpu.VMEM((4, 1456, 128), BF16),
            pltpu.VMEM((2, 3, 736, 128), BF16),
            pltpu.VMEM((768, 720), BF16),
            pltpu.VMEM((1, 1024), F32),
            pltpu.SemaphoreType.DMA((6,)),
            pltpu.SemaphoreType.DMA((2, 8, 2)),
            pltpu.SemaphoreType.DMA((2, 8, 2)),
            pltpu.SemaphoreType.DMA((3, 4, 6)),
            pltpu.SemaphoreType.DMA((3, 4, 6)),
            pltpu.SemaphoreType.DMA,
            pltpu.SemaphoreType.DMA,
            pltpu.SemaphoreType.DMA((2, 3)),
            pltpu.SemaphoreType.DMA((2, 3)),
        ],
        compiler_params=pltpu.CompilerParams(
            collective_id=0, has_side_effects=True, vmem_limit_bytes=64 * 1024 * 1024
        ),
    )(x, og, ids, probs, wg, wu, wd)


def on_device(tokens, out_grad, expert_ids, probs, w_gate, w_up, w_down):
    down, gate, up, ig, routed = layer(
        tokens.T, out_grad.T, expert_ids.T, probs.T, w_gate[0], w_up[0], w_down[0]
    )
    return ig.T, routed.T, gate[None], up[None], down[None]


def solution(mesh):
    tok = P(("dp", "expert"), None)
    w = P("expert", None, None)
    g = P("expert", "dp", None)
    return jax.shard_map(
        on_device,
        mesh=mesh,
        in_specs=(tok, tok, tok, tok, w, w, w),
        out_specs=(tok, tok, g, g, g),
        check_vma=False,
    )
```

```python
import functools

import jax
import jax.numpy as jnp
from jax import lax
from jax.experimental import pallas as pl
from jax.experimental.pallas import tpu as pltpu
from jax.sharding import PartitionSpec as P

BF16, F32 = jnp.bfloat16, jnp.float32
MESH = pl.DeviceIdType.MESH
NT = (((1,), (1,)), ((), ()))
NN = (((1,), (0,)), ((), ()))
CHIP = 256


def mod4(v):
    return lax.rem(v + 8, 4)


def place():
    dp = lax.axis_index("dp")
    ex = lax.axis_index("expert")
    return dp // 4, lax.rem(dp, 4), ex // 2, lax.rem(ex, 2)


def kernel(
    x_h, og_h, ids, probs, wg_h, wu_h, wd_h,
    out, ig_out, routed,
    xg, og, xp, hp, gg, ug, wa, wb, terms, r1, r2, sib, rx, spread, racc,
    load, g_send, g_recv, s_send, s_recv, b_send, b_recv, x_send, x_recv,
):
    y, z, x, c = place()
    dp, ex = y * 4 + z, x * 2 + c

    def at(dp_to=None, ex_to=None):
        return (dp if dp_to is None else dp_to, ex if ex_to is None else ex_to)

    def along(axis, d):
        if axis == "y":
            return at(dp_to=mod4(y + d) * 4 + z)
        if axis == "z":
            return at(dp_to=y * 4 + mod4(z + d))
        return at(ex_to=mod4(x + d) * 2 + c)


    own_x = pltpu.make_async_copy(x_h, xg.at[x, c, 0:1440], load.at[0])
    own_og = pltpu.make_async_copy(og_h, og.at[x, c], load.at[1])
    load_g = pltpu.make_async_copy(wg_h, wa, load.at[2])
    load_u = pltpu.make_async_copy(wu_h, wb, load.at[3])
    load_d = pltpu.make_async_copy(wd_h, wa, load.at[4])
    load_g2 = pltpu.make_async_copy(wg_h, wa, load.at[5])
    for copy in (own_x, own_og, load_g, load_u):
        copy.start()
    sibling = at(ex_to=x * 2 + 1 - c)
    barrier = pltpu.get_barrier_semaphore()
    for to in [along(a, d) for a in "xyz" for d in (1, -1)] + [sibling]:
        pl.semaphore_signal(barrier, inc=1, device_id=to, device_id_type=MESH)

    left, right, far = mod4(x - 1), mod4(x + 1), mod4(x + 2)

    def hop(a, kind, half, got=False):
        buf = (xg, og)[a]
        rows = slice(0, 768) if half == 0 else slice(768, 1456 if a == 0 else 1440)
        n, sent, arrived, to = {
            "right": (0, x, left, along("x", 1)),
            "left": (1, x, right, along("x", -1)),
            "pass_right": (2, left, far, along("x", 1)),
            "pass_left": (3, right, far, along("x", -1)),
            "core_own": (4, x, x, sibling),
            "core_left": (5, left, left, sibling),
            "core_right": (6, right, right, sibling),
            "core_far": (7, far, far, sibling),
        }[kind]
        core = 1 - c if got and n >= 4 else c
        block = buf.at[arrived if got else sent, core, rows]
        return pltpu.make_async_remote_copy(
            src_ref=block, dst_ref=block, send_sem=g_send.at[a, n, half],
            recv_sem=g_recv.at[a, n, half], device_id=to, device_id_type=MESH,
        )

    sent = []

    def send(a, *names):
        for name, half in names:
            hop(a, name, half).start()
            sent.append((a, name, half))

    def got(a, *names):
        for name, half in names:
            hop(a, name, half, got=True).wait_recv()

    def both(name):
        return (name, 0), (name, 1)

    rowid = lax.broadcasted_iota(jnp.int32, (16, 128), 0)
    dense = jnp.zeros((16, 128), F32)
    for k in range(4):
        dense = dense + jnp.where(ids[k : k + 1, :] == rowid, probs[k : k + 1, :].astype(F32), 0.0)
    xg[x, c, 1440:1456, :] = dense.astype(BF16)
    own_x.wait()
    pl.semaphore_wait(barrier, 7)
    send(0, ("right", 0), ("left", 1), *both("core_own"), ("right", 1), ("left", 0))

    row = lax.broadcasted_iota(jnp.int32, (768, 720), 0)
    col = lax.broadcasted_iota(jnp.int32, (768, 720), 1)
    rest = row - 384
    above = lax.div(row, 192) * 360 + lax.div(lax.rem(row, 192), 48) * 90 + lax.rem(row, 48)
    below = lax.rem(lax.div(rest, 48), 2) * 360 + lax.div(rest, 96) * 90 + 48 + lax.rem(rest, 48)
    kept = lax.rem(row, 48) < 42
    picked = ((row < 384) & (above == col)) | ((row >= 384) & kept & (below == col))
    spread[...] = jnp.where(picked, 1.0, 0.0).astype(BF16)

    def flip(w, m):
        for k in range(4):
            n = 384 if k < 3 else 288
            t = w[:, k * 384 : k * 384 + n].T
            for h in range(2):
                r0, r1_ = max(k * 384, h * 720), min(k * 384 + n, h * 720 + 720)
                if r0 < r1_:
                    part = t[r0 - k * 384 : r1_ - k * 384]
                    to = slice(r0 - h * 720, r1_ - h * 720)
                    terms[m, 2 * h, to, :] = part[:, 0:768]
                    terms[m, 2 * h + 1, to, 0:672] = part[:, 768:1440]

    def lanes_of(chip):
        return pl.ds(pl.multiple_of(chip * CHIP, CHIP), CHIP)

    def gate_of(chip):
        parts = []
        for k in range(2):
            rows = xg[chip, k, 1440:1456, :].astype(F32)
            parts.append(jnp.sum(jnp.where(rowid == ex, rows, 0.0), axis=0, keepdims=True))
        return jnp.concatenate(parts, axis=1)

    def place_rows(to, h, v, lanes):
        t = lax.dot_general(spread[...], v, NN, preferred_element_type=F32).astype(BF16)
        to[h * 384 : h * 384 + 384, lanes] = t[0:384]
        for k in range(4):
            r0 = 768 + k * 192 + h * 96
            to[r0 : r0 + 96, lanes] = t[384 + k * 96 : 480 + k * 96]

    def forward(chip):
        lanes = lanes_of(chip)
        gate = gate_of(chip)
        cols = jnp.concatenate([xg[chip, 0, 0:1440, :], xg[chip, 1, 0:1440, :]], axis=1)
        for h in range(2):
            rows = slice(h * 720, h * 720 + 720)
            g, u = [
                lax.dot_general(
                    terms[m, 2 * h, 0:720, :], cols[0:768], NN, preferred_element_type=F32
                )
                + lax.dot_general(
                    terms[m, 2 * h + 1, 0:720, 0:672], cols[768:1440], NN, preferred_element_type=F32
                )
                for m in range(2)
            ]
            s = 0.5 * jnp.tanh(0.5 * g) + 0.5
            gs = g * s
            hidden = gs * u
            gg[rows, lanes] = (u * (s + gs * (1.0 - s))).astype(BF16)
            ug[rows, lanes] = gs.astype(BF16)
            xp[rows, lanes] = hidden.astype(BF16)
            place_rows(hp, h, (gate * hidden).astype(BF16), lanes)

    def gradient(chip):
        lanes = lanes_of(chip)
        gate = gate_of(chip)
        cols = jnp.concatenate([og[chip, 0], og[chip, 1]], axis=1)
        total = jnp.zeros((1, CHIP), F32)
        for h in range(2):
            rows = slice(h * 720, h * 720 + 720)
            a = lax.dot_general(wa[rows, :], cols, NN, preferred_element_type=F32)
            pa = gate * a
            gg[rows, lanes] = (pa * gg[rows, lanes].astype(F32)).astype(BF16)
            ug[rows, lanes] = (pa * ug[rows, lanes].astype(F32)).astype(BF16)
            hidden = xp[rows, lanes].astype(F32)
            total = total + jnp.sum(hidden * a, axis=0, keepdims=True)
        racc[:, lanes] = total

    def widen(chip):
        for h in range(2):
            rows = slice(h * 720, h * 720 + 720)
            v = jnp.concatenate([xg[chip, 0, rows, :], xg[chip, 1, rows, :]], axis=1)
            place_rows(xp, h, v, lanes_of(chip))

    streams = [("y", 1), ("y", -1), ("z", 1), ("z", -1)]
    rings = {"y": y, "z": z}

    def chunk(index):
        return pl.ds(pl.multiple_of(index * 192, 64), 192)

    def term(m, s):
        r0 = (s // 2) * 768
        a = (hp if m == 0 else xp)[r0 : r0 + 768, :]
        cols = slice(0, 768) if s % 2 == 0 else slice(768, 1440)
        if m == 0:
            b = jnp.concatenate([og[k // 2, k % 2, cols, :] for k in range(8)], axis=1)
        else:
            b = (gg, ug)[m - 1][cols, :]
        t = lax.dot_general(a, b, NT, preferred_element_type=F32).astype(BF16)
        terms[m, s, :, 0 : t.shape[1]] = t

    def first_copy(m, s, t):
        axis, d = streams[s]
        mine = terms.at[m, s, chunk(mod4(rings[axis] - d))]
        return pltpu.make_async_remote_copy(
            src_ref=mine if t == 0 else r1.at[m, s, t - 1], dst_ref=r1.at[m, s, t],
            send_sem=s_send.at[m, s, t], recv_sem=s_recv.at[m, s, t],
            device_id=along(axis, d), device_id_type=MESH,
        )

    def share(index):
        return pl.ds(pl.multiple_of(index * 48, 16), 48)

    def second_copy(m, s, t):
        axis, d = streams[s]
        other = "z" if axis == "y" else "y"
        src = r1.at[m, s, 2, share(mod4(rings[other] - d))] if t == 0 else r2.at[m, s, t - 1]
        return pltpu.make_async_remote_copy(
            src_ref=src, dst_ref=r2.at[m, s, t], send_sem=s_send.at[m, s, 3 + t],
            recv_sem=s_recv.at[m, s, 3 + t], device_id=along(other, d), device_id_type=MESH,
        )

    def start(m):
        for s in range(4):
            term(m, s)
            first_copy(m, s, 0).start()

    def advance(m, stage):
        for s in range(4):
            axis, d = streams[s]
            if stage < 3:
                first_copy(m, s, stage).wait_recv()
                mine = terms[m, s, chunk(mod4(rings[axis] - d * (2 + stage))), :]
                r1[m, s, stage] = r1[m, s, stage] + mine
                if stage < 2:
                    first_copy(m, s, stage + 1).start()
                else:
                    second_copy(m, s, 0).start()
            else:
                t = stage - 3
                other = "z" if axis == "y" else "y"
                second_copy(m, s, t).wait_recv()
                mine = r1[m, s, 2, share(mod4(rings[other] - d * (2 + t))), :].astype(F32)
                total = r2[m, s, t].astype(F32) + mine
                if t < 2:
                    r2[m, s, t] = total.astype(BF16)
                    second_copy(m, s, t + 1).start()
                else:
                    n = 48 if axis == "y" else 42
                    r0 = 0 if axis == "y" else 48
                    if s % 2 == 0:
                        out[m, r0 : r0 + n, 0, 0:768] = total[0:n]
                    else:
                        out[m, r0 : r0 + n, 0, 768:1440] = total[0:n, 0:672]

    def ig_tile(chip, h):
        rows = slice(h * 720, h * 720 + 720)
        lanes = slice(chip * CHIP, chip * CHIP + CHIP)
        t = lax.dot_general(wa[rows, :], gg[:, lanes], NN, preferred_element_type=F32)
        t = t + lax.dot_general(wb[rows, :], ug[:, lanes], NN, preferred_element_type=F32)
        t = t.astype(BF16)
        xg[chip, 0, rows, :] = t[:, 0:128]
        xg[chip, 1, rows, :] = t[:, 128:256]

    sib_copy = pltpu.make_async_remote_copy(
        src_ref=xg.at[:, 1 - c], dst_ref=sib, send_sem=b_send, recv_sem=b_recv,
        device_id=sibling, device_id_type=MESH,
    )
    halves = ((1, 0, 720), (-1, 720, 736))

    def x_copy(h, t):
        d, lo, n = halves[h]
        src = sib.at[mod4(x - d), lo : lo + n] if t == 0 else rx.at[h, t - 1, 0:n]
        return pltpu.make_async_remote_copy(
            src_ref=src, dst_ref=rx.at[h, t, 0:n], send_sem=x_send.at[h, t],
            recv_sem=x_recv.at[h, t], device_id=along("x", d), device_id_type=MESH,
        )

    def ig_pair():
        sib_copy.wait_recv()
        for k in range(4):
            sib[k] = sib[k] + xg[k, c]
        for h in range(2):
            x_copy(h, 0).start()

    def ig_step(t):
        for h in range(2):
            d, lo, n = halves[h]
            x_copy(h, t).wait_recv()
            own = sib[mod4(x - d * (2 + t)), lo : lo + n]
            if t < 2:
                rx[h, t, 0:n] = rx[h, t, 0:n] + own
                x_copy(h, t + 1).start()
            else:
                total = rx[h, t, 0:n].astype(F32) + own.astype(F32)
                ig_out[lo : lo + 720, :] = total[0:720].astype(BF16)
                if h == 1:
                    for k in range(4):
                        mine = jnp.where(ids[k : k + 1, :] == rowid, total[720:736], 0.0)
                        routed[k : k + 1, :] = jnp.sum(mine, axis=0, keepdims=True).astype(BF16)

    load_g.wait()
    flip(wa, 0)
    load_d.start()
    load_u.wait()
    flip(wb, 1)
    got(0, *both("core_own"))
    forward(x)
    got(0, ("right", 0))
    send(0, ("pass_right", 0))
    got(0, ("left", 1))
    send(0, ("pass_left", 1))
    own_og.wait()
    send(1, *both("right"), *both("left"), *both("core_own"))
    got(0, ("right", 1))
    send(0, *both("core_left"))
    got(0, ("left", 0))
    send(0, *both("core_right"))
    load_d.wait()
    got(1, *both("core_own"))
    gradient(x)
    got(0, *both("core_left"))
    forward(left)
    got(0, *both("core_right"))
    forward(right)
    got(0, ("pass_right", 0), ("pass_left", 1))
    send(0, *both("core_far"))
    got(1, ("right", 0))
    send(1, ("pass_right", 0))
    got(1, ("left", 1))
    send(1, ("pass_left", 1))
    got(1, ("right", 1))
    send(1, *both("core_left"))
    got(1, ("left", 0))
    send(1, *both("core_right"))
    got(0, *both("core_far"))
    forward(far)
    got(1, *both("core_left"))
    gradient(left)
    got(1, *both("core_right"))
    gradient(right)
    got(1, ("pass_right", 0), ("pass_left", 1))
    send(1, *both("core_far"))
    widen(x)
    widen(left)
    widen(right)
    got(1, *both("core_far"))
    start(0)
    gradient(far)
    load_g2.start()
    widen(far)
    start(1)
    advance(0, 0)
    start(2)
    for a, name, half in sent:
        if a == 0:
            hop(a, name, half).wait_send()
    for b in range(8):
        part = jnp.broadcast_to(racc[:, b * 128 : (b + 1) * 128], (16, 128))
        xg[b // 2, b % 2, 1440:1456, :] = jnp.where(rowid == ex, part, 0.0).astype(BF16)
    advance(1, 0)
    load_g2.wait()
    ig_tile(0, 0)
    advance(0, 1)
    ig_tile(0, 1)
    ig_tile(1, 0)
    advance(2, 0)
    ig_tile(1, 1)
    ig_tile(2, 0)
    ig_tile(2, 1)
    advance(1, 1)
    ig_tile(3, 0)
    ig_tile(3, 1)
    sib_copy.start()
    advance(0, 2)
    advance(2, 1)
    ig_pair()
    advance(0, 3)
    advance(1, 2)
    advance(0, 4)
    ig_step(0)
    advance(1, 3)
    advance(2, 2)
    advance(0, 5)
    advance(1, 4)
    ig_step(1)
    advance(2, 3)
    advance(1, 5)
    ig_step(2)
    advance(2, 4)
    advance(2, 5)
    sib_copy.wait_send()
    for h in range(2):
        for t in range(3):
            x_copy(h, t).wait_send()
    for m in range(3):
        for s in range(4):
            for t in range(3):
                first_copy(m, s, t).wait_send()
                second_copy(m, s, t).wait_send()
    for a, name, half in sent:
        if a == 1:
            hop(a, name, half).wait_send()


def layer(x, og, ids, probs, wg, wu, wd):
    hbm = pl.BlockSpec(memory_space=pl.ANY)
    vmem = pl.BlockSpec(memory_space=pltpu.VMEM)
    return pl.pallas_call(
        kernel,
        out_shape=(
            jax.ShapeDtypeStruct((3, 90, 1, 1440), F32),
            jax.ShapeDtypeStruct((1440, 128), BF16),
            jax.ShapeDtypeStruct((4, 128), BF16),
        ),
        in_specs=[hbm, hbm, vmem, vmem, hbm, hbm, hbm],
        out_specs=(vmem,) * 3,
        scratch_shapes=[
            pltpu.VMEM((4, 2, 1456, 128), BF16),
            pltpu.VMEM((4, 2, 1440, 128), BF16),
            pltpu.VMEM((1536, 1024), BF16),
            pltpu.VMEM((1536, 1024), BF16),
            pltpu.VMEM((1440, 1024), BF16),
            pltpu.VMEM((1440, 1024), BF16),
            pltpu.VMEM((1440, 1440), BF16),
            pltpu.VMEM((1440, 1440), BF16),
            pltpu.VMEM((3, 4, 768, 768), BF16),
            pltpu.VMEM((3, 4, 3, 192, 768), BF16),
            pltpu.VMEM((3, 4, 3, 48, 768), BF16),
            pltpu.VMEM((4, 1456, 128), BF16),
            pltpu.VMEM((2, 3, 736, 128), BF16),
            pltpu.VMEM((768, 720), BF16),
            pltpu.VMEM((1, 1024), F32),
            pltpu.SemaphoreType.DMA((6,)),
            pltpu.SemaphoreType.DMA((2, 8, 2)),
            pltpu.SemaphoreType.DMA((2, 8, 2)),
            pltpu.SemaphoreType.DMA((3, 4, 6)),
            pltpu.SemaphoreType.DMA((3, 4, 6)),
            pltpu.SemaphoreType.DMA,
            pltpu.SemaphoreType.DMA,
            pltpu.SemaphoreType.DMA((2, 3)),
            pltpu.SemaphoreType.DMA((2, 3)),
        ],
        compiler_params=pltpu.CompilerParams(
            collective_id=0, has_side_effects=True, vmem_limit_bytes=64 * 1024 * 1024
        ),
    )(x, og, ids, probs, wg, wu, wd)


def on_device(tokens, out_grad, expert_ids, probs, w_gate, w_up, w_down):
    out, ig, routed = layer(
        tokens.T, out_grad.T, expert_ids.T, probs.T, w_gate[0], w_up[0], w_down[0]
    )
    down, gate, up = [jnp.transpose(out[m], (1, 0, 2)) for m in range(3)]
    return ig.T, routed.T, gate, up, down


def solution(mesh):
    tok = P(("dp", "expert"), None)
    w = P("expert", None, None)
    g = P("expert", "dp", None)
    return jax.shard_map(
        on_device,
        mesh=mesh,
        in_specs=(tok, tok, tok, tok, w, w, w),
        out_specs=(tok, tok, g, g, g),
        check_vma=False,
    )
```

```python
import functools

import jax
import jax.numpy as jnp
from jax import lax
from jax.experimental import pallas as pl
from jax.experimental.pallas import tpu as pltpu
from jax.sharding import PartitionSpec as P

BF16, F32 = jnp.bfloat16, jnp.float32
MESH = pl.DeviceIdType.MESH
NT = (((1,), (1,)), ((), ()))
NN = (((1,), (0,)), ((), ()))
CHIP = 256


def mod4(v):
    return lax.rem(v + 8, 4)


def place():
    dp = lax.axis_index("dp")
    ex = lax.axis_index("expert")
    return dp // 4, lax.rem(dp, 4), ex // 2, lax.rem(ex, 2)


def kernel(
    x_h, og_h, ids, probs, wg_h, wu_h, wd_h,
    out, ig_out, routed,
    xg, og, xp, hp, gu, wa, wb, terms, r1, r2, sib, rx, spread, racc,
    load, g_send, g_recv, s_send, s_recv, b_send, b_recv, x_send, x_recv,
):
    y, z, x, c = place()
    dp, ex = y * 4 + z, x * 2 + c

    def at(dp_to=None, ex_to=None):
        return (dp if dp_to is None else dp_to, ex if ex_to is None else ex_to)

    def along(axis, d):
        if axis == "y":
            return at(dp_to=mod4(y + d) * 4 + z)
        if axis == "z":
            return at(dp_to=y * 4 + mod4(z + d))
        return at(ex_to=mod4(x + d) * 2 + c)


    own_x = pltpu.make_async_copy(x_h, xg.at[x, c, 0:1440], load.at[0])
    own_og = pltpu.make_async_copy(og_h, og.at[x, c, 0:1440], load.at[1])
    load_g = pltpu.make_async_copy(wg_h, wa, load.at[2])
    load_u = pltpu.make_async_copy(wu_h, wb, load.at[3])
    load_d = pltpu.make_async_copy(wd_h, wa, load.at[4])
    load_g2 = pltpu.make_async_copy(wg_h, wa, load.at[5])
    for copy in (own_x, own_og, load_g, load_u):
        copy.start()
    sibling = at(ex_to=x * 2 + 1 - c)
    barrier = pltpu.get_barrier_semaphore()
    for to in [along(a, d) for a in "xyz" for d in (1, -1)] + [sibling]:
        pl.semaphore_signal(barrier, inc=1, device_id=to, device_id_type=MESH)

    left, right, far = mod4(x - 1), mod4(x + 1), mod4(x + 2)

    def hop(a, kind, half, got=False):
        buf = (xg, og)[a]
        rows = slice(0, 768) if half == 0 else slice(768, 1456 if a == 0 else 1440)
        n, sent, arrived, to = {
            "right": (0, x, left, along("x", 1)),
            "left": (1, x, right, along("x", -1)),
            "pass_right": (2, left, far, along("x", 1)),
            "pass_left": (3, right, far, along("x", -1)),
            "core_own": (4, x, x, sibling),
            "core_left": (5, left, left, sibling),
            "core_right": (6, right, right, sibling),
            "core_far": (7, far, far, sibling),
        }[kind]
        core = 1 - c if got and n >= 4 else c
        block = buf.at[arrived if got else sent, core, rows]
        return pltpu.make_async_remote_copy(
            src_ref=block, dst_ref=block, send_sem=g_send.at[a, n, half],
            recv_sem=g_recv.at[a, n, half], device_id=to, device_id_type=MESH,
        )

    sent = []

    def send(a, *names):
        for name, half in names:
            hop(a, name, half).start()
            sent.append((a, name, half))

    def got(a, *names):
        for name, half in names:
            hop(a, name, half, got=True).wait_recv()

    def both(name):
        return (name, 0), (name, 1)

    rowid = lax.broadcasted_iota(jnp.int32, (16, 128), 0)
    dense = jnp.zeros((16, 128), F32)
    for k in range(4):
        dense = dense + jnp.where(ids[k : k + 1, :] == rowid, probs[k : k + 1, :].astype(F32), 0.0)
    xg[x, c, 1440:1456, :] = dense.astype(BF16)
    own_x.wait()
    pl.semaphore_wait(barrier, 7)
    send(0, ("right", 0), ("left", 1), *both("core_own"), ("right", 1), ("left", 0))

    row = lax.broadcasted_iota(jnp.int32, (768, 720), 0)
    col = lax.broadcasted_iota(jnp.int32, (768, 720), 1)
    rest = row - 384
    above = lax.div(row, 192) * 360 + lax.div(lax.rem(row, 192), 48) * 90 + lax.rem(row, 48)
    below = lax.rem(lax.div(rest, 48), 2) * 360 + lax.div(rest, 96) * 90 + 48 + lax.rem(rest, 48)
    kept = lax.rem(row, 48) < 42
    picked = ((row < 384) & (above == col)) | ((row >= 384) & kept & (below == col))
    spread[...] = jnp.where(picked, 1.0, 0.0).astype(BF16)

    def flip(w, m):
        for k in range(4):
            n = 384 if k < 3 else 288
            t = w[:, k * 384 : k * 384 + n].T
            for h in range(2):
                r0, r1_ = max(k * 384, h * 720), min(k * 384 + n, h * 720 + 720)
                if r0 < r1_:
                    part = t[r0 - k * 384 : r1_ - k * 384]
                    to = slice(r0 - h * 720, r1_ - h * 720)
                    terms[m, 2 * h, to, :] = part[:, 0:768]
                    terms[m, 2 * h + 1, to, 0:672] = part[:, 768:1440]

    def lanes_of(chip):
        return pl.ds(pl.multiple_of(chip * CHIP, CHIP), CHIP)

    def gate_of(chip):
        parts = []
        for k in range(2):
            rows = xg[chip, k, 1440:1456, :].astype(F32)
            parts.append(jnp.sum(jnp.where(rowid == ex, rows, 0.0), axis=0, keepdims=True))
        return jnp.concatenate(parts, axis=1)

    def place_rows(to, h, v, lanes):
        t = lax.dot_general(spread[...], v, NN, preferred_element_type=F32).astype(BF16)
        to[h * 384 : h * 384 + 384, lanes] = t[0:384]
        for k in range(4):
            r0 = 768 + k * 192 + h * 96
            to[r0 : r0 + 96, lanes] = t[384 + k * 96 : 480 + k * 96]

    def forward(chip):
        lanes = lanes_of(chip)
        gate = gate_of(chip)
        cols = jnp.concatenate([xg[chip, 0, 0:1440, :], xg[chip, 1, 0:1440, :]], axis=1)
        for h in range(2):
            rows = slice(h * 720, h * 720 + 720)
            g, u = [
                lax.dot_general(
                    terms[m, 2 * h, 0:720, :], cols[0:768], NN, preferred_element_type=F32
                )
                + lax.dot_general(
                    terms[m, 2 * h + 1, 0:720, 0:672], cols[768:1440], NN, preferred_element_type=F32
                )
                for m in range(2)
            ]
            s = 0.5 * jnp.tanh(0.5 * g) + 0.5
            gs = g * s
            hidden = gs * u
            gu[0, rows, lanes] = (u * (s + gs * (1.0 - s))).astype(BF16)
            gu[1, rows, lanes] = gs.astype(BF16)
            xp[rows, lanes] = hidden.astype(BF16)
            place_rows(hp, h, (gate * hidden).astype(BF16), lanes)

    def gradient(chip):
        lanes = lanes_of(chip)
        gate = gate_of(chip)
        cols = jnp.concatenate([og[chip, 0, 0:1440, :], og[chip, 1, 0:1440, :]], axis=1)
        total = jnp.zeros((1, CHIP), F32)
        for h in range(2):
            rows = slice(h * 720, h * 720 + 720)
            a = lax.dot_general(wa[rows, :], cols, NN, preferred_element_type=F32)
            pa = gate * a
            gu[0, rows, lanes] = (pa * gu[0, rows, lanes].astype(F32)).astype(BF16)
            gu[1, rows, lanes] = (pa * gu[1, rows, lanes].astype(F32)).astype(BF16)
            hidden = xp[rows, lanes].astype(F32)
            total = total + jnp.sum(hidden * a, axis=0, keepdims=True)
        racc[:, lanes] = total

    def widen(chip):
        for h in range(2):
            rows = slice(h * 720, h * 720 + 720)
            v = jnp.concatenate([xg[chip, 0, rows, :], xg[chip, 1, rows, :]], axis=1)
            place_rows(xp, h, v, lanes_of(chip))

    def way(s):
        first = 1 - s // 2
        d = 1 - 2 * lax.rem(s, 2)
        return first, d

    def step_to(on_y, d):
        return at(dp_to=mod4(y + d * on_y) * 4 + mod4(z + d * (1 - on_y)))

    def chunk(index):
        return pl.ds(pl.multiple_of(index * 192, 64), 192)

    def share(index):
        return pl.ds(pl.multiple_of(index * 48, 16), 48)

    def first_copy(m, s, t):
        on_y, d = way(s)
        pos = y * on_y + z * (1 - on_y)
        src = terms.at[m, s, chunk(mod4(pos - d))] if t == 0 else r1.at[m, s, t - 1]
        return pltpu.make_async_remote_copy(
            src_ref=src, dst_ref=r1.at[m, s, t], send_sem=s_send.at[m, s, t],
            recv_sem=s_recv.at[m, s, t], device_id=step_to(on_y, d), device_id_type=MESH,
        )

    def second_copy(m, s, t):
        on_y, d = way(s)
        pos = z * on_y + y * (1 - on_y)
        src = r1.at[m, s, 2, share(mod4(pos - d))] if t == 0 else r2.at[m, s, t - 1]
        return pltpu.make_async_remote_copy(
            src_ref=src, dst_ref=r2.at[m, s, t], send_sem=s_send.at[m, s, 3 + t],
            recv_sem=s_recv.at[m, s, 3 + t], device_id=step_to(1 - on_y, d), device_id_type=MESH,
        )

    def start(m):
        def body(s, carry):
            r0 = pl.multiple_of((s // 2) * 768, 768)
            c0 = pl.multiple_of(lax.rem(s, 2) * 768, 768)
            a = (hp if m == 0 else xp)[pl.ds(r0, 768), :]
            if m == 0:
                parts = [og[k // 2, k % 2, pl.ds(c0, 768), :] for k in range(8)]
                b = jnp.concatenate(parts, axis=1)
            else:
                b = gu[m - 1, pl.ds(c0, 768), :]
            terms[m, s] = lax.dot_general(a, b, NT, preferred_element_type=F32).astype(BF16)
            first_copy(m, s, 0).start()
            return carry

        lax.fori_loop(0, 4, body, 0)

    def advance(m, stage):
        def body(s, carry):
            on_y, d = way(s)
            if stage < 3:
                pos = y * on_y + z * (1 - on_y)
                first_copy(m, s, stage).wait_recv()
                mine = terms[m, s, chunk(mod4(pos - d * (2 + stage))), :]
                r1[m, s, stage] = r1[m, s, stage] + mine
                if stage < 2:
                    first_copy(m, s, stage + 1).start()
                else:
                    second_copy(m, s, 0).start()
                return carry
            t = stage - 3
            pos = z * on_y + y * (1 - on_y)
            second_copy(m, s, t).wait_recv()
            mine = r1[m, s, 2, share(mod4(pos - d * (2 + t))), :].astype(F32)
            total = r2[m, s, t].astype(F32) + mine
            if t < 2:
                r2[m, s, t] = total.astype(BF16)
                second_copy(m, s, t + 1).start()
            else:
                r0, n = 48 * (s // 2), 48 - 6 * (s // 2)
                lanes = (s % 2) * 768
                width = 768 - 96 * (s % 2)
                out[m, r0 : r0 + n, 0, lanes : lanes + width] = total[0:n, 0:width]
            return carry

        if stage < 5:
            lax.fori_loop(0, 4, body, 0)
        else:
            for s in range(4):
                body(s, 0)

    def ig_chip(chip):
        lanes = slice(chip * CHIP, chip * CHIP + CHIP)

        def body(h, carry):
            rows = pl.ds(pl.multiple_of(h * 720, 16), 720)
            t = lax.dot_general(wa[rows, :], gu[0, 0:1440, lanes], NN, preferred_element_type=F32)
            u = lax.dot_general(wb[rows, :], gu[1, 0:1440, lanes], NN, preferred_element_type=F32)
            t = (t + u).astype(BF16)
            xg[chip, 0, rows, :] = t[:, 0:128]
            xg[chip, 1, rows, :] = t[:, 128:256]
            return carry

        lax.fori_loop(0, 2, body, 0)

    sib_copy = pltpu.make_async_remote_copy(
        src_ref=xg.at[:, 1 - c], dst_ref=sib, send_sem=b_send, recv_sem=b_recv,
        device_id=sibling, device_id_type=MESH,
    )
    halves = ((1, 0, 720), (-1, 720, 736))

    def x_copy(h, t):
        d, lo, n = halves[h]
        src = sib.at[mod4(x - d), lo : lo + n] if t == 0 else rx.at[h, t - 1, 0:n]
        return pltpu.make_async_remote_copy(
            src_ref=src, dst_ref=rx.at[h, t, 0:n], send_sem=x_send.at[h, t],
            recv_sem=x_recv.at[h, t], device_id=along("x", d), device_id_type=MESH,
        )

    def ig_pair():
        sib_copy.wait_recv()
        for k in range(4):
            sib[k] = sib[k] + xg[k, c]
        for h in range(2):
            x_copy(h, 0).start()

    def ig_step(t):
        for h in range(2):
            d, lo, n = halves[h]
            x_copy(h, t).wait_recv()
            own = sib[mod4(x - d * (2 + t)), lo : lo + n]
            if t < 2:
                rx[h, t, 0:n] = rx[h, t, 0:n] + own
                x_copy(h, t + 1).start()
            else:
                total = rx[h, t, 0:n].astype(F32) + own.astype(F32)
                ig_out[lo : lo + 720, :] = total[0:720].astype(BF16)
                if h == 1:
                    for k in range(4):
                        mine = jnp.where(ids[k : k + 1, :] == rowid, total[720:736], 0.0)
                        routed[k : k + 1, :] = jnp.sum(mine, axis=0, keepdims=True).astype(BF16)

    load_g.wait()
    flip(wa, 0)
    load_d.start()
    load_u.wait()
    flip(wb, 1)

    def chip_at(i):
        return mod4(x + i + (i // 2) * (1 - 2 * lax.rem(i, 2)))

    def forwards(i, carry):
        @pl.when(i == 0)
        def _():
            got(0, *both("core_own"))

        @pl.when(i == 1)
        def _():
            got(0, ("right", 0))
            send(0, ("pass_right", 0))
            got(0, ("left", 1))
            send(0, ("pass_left", 1))
            own_og.wait()
            send(1, *both("right"), *both("left"), *both("core_own"))
            got(0, ("left", 0))
            send(0, *both("core_right"))
            got(0, ("right", 1))
            send(0, *both("core_left"))
            got(0, *both("core_right"))

        @pl.when(i == 2)
        def _():
            got(0, *both("core_left"))

        @pl.when(i == 3)
        def _():
            got(0, ("pass_right", 0), ("pass_left", 1))
            send(0, *both("core_far"))
            got(1, ("right", 0))
            send(1, ("pass_right", 0))
            got(1, ("left", 1))
            send(1, ("pass_left", 1))
            got(1, ("left", 0))
            send(1, *both("core_right"))
            got(1, ("right", 1))
            send(1, *both("core_left"))
            got(0, *both("core_far"))

        forward(chip_at(i))
        return carry

    def widens(i, carry):
        widen(chip_at(i))
        return carry

    def gradients(i, carry):
        @pl.when(i == 0)
        def _():
            load_d.wait()
            got(1, *both("core_own"))

        @pl.when(i == 1)
        def _():
            got(1, *both("core_right"))

        @pl.when(i == 2)
        def _():
            got(1, *both("core_left"))

        @pl.when(i == 3)
        def _():
            got(1, ("pass_right", 0), ("pass_left", 1))
            send(1, *both("core_far"))
            lax.fori_loop(0, 3, widens, 0)
            got(1, *both("core_far"))
            start(0)

        gradient(chip_at(i))
        return carry

    lax.fori_loop(0, 4, forwards, 0)
    lax.fori_loop(0, 4, gradients, 0)
    load_g2.start()
    lax.fori_loop(3, 4, widens, 0)
    start(1)
    advance(0, 0)
    start(2)
    for a, name, half in sent:
        if a == 0:
            hop(a, name, half).wait_send()
    for b in range(8):
        part = jnp.broadcast_to(racc[:, b * 128 : (b + 1) * 128], (16, 128))
        xg[b // 2, b % 2, 1440:1456, :] = jnp.where(rowid == ex, part, 0.0).astype(BF16)
    advance(1, 0)
    load_g2.wait()
    ig_chip(0)
    advance(0, 1)
    ig_chip(1)
    advance(2, 0)
    ig_chip(2)
    advance(1, 1)
    ig_chip(3)
    sib_copy.start()
    advance(0, 2)
    advance(2, 1)
    ig_pair()
    advance(0, 3)
    advance(1, 2)
    advance(0, 4)
    ig_step(0)
    advance(1, 3)
    advance(2, 2)
    advance(0, 5)
    advance(1, 4)
    ig_step(1)
    advance(2, 3)
    advance(1, 5)
    ig_step(2)
    advance(2, 4)
    advance(2, 5)
    sib_copy.wait_send()
    for h in range(2):
        for t in range(3):
            x_copy(h, t).wait_send()
    for m in range(3):
        for s in range(4):
            for t in range(3):
                first_copy(m, s, t).wait_send()
                second_copy(m, s, t).wait_send()
    for a, name, half in sent:
        if a == 1:
            hop(a, name, half).wait_send()


def layer(x, og, ids, probs, wg, wu, wd):
    hbm = pl.BlockSpec(memory_space=pl.ANY)
    vmem = pl.BlockSpec(memory_space=pltpu.VMEM)
    return pl.pallas_call(
        kernel,
        out_shape=(
            jax.ShapeDtypeStruct((3, 90, 1, 1440), F32),
            jax.ShapeDtypeStruct((1440, 128), BF16),
            jax.ShapeDtypeStruct((4, 128), BF16),
        ),
        in_specs=[hbm, hbm, vmem, vmem, hbm, hbm, hbm],
        out_specs=(vmem,) * 3,
        scratch_shapes=[
            pltpu.VMEM((4, 2, 1456, 128), BF16),
            pltpu.VMEM((4, 2, 1536, 128), BF16),
            pltpu.VMEM((1536, 1024), BF16),
            pltpu.VMEM((1536, 1024), BF16),
            pltpu.VMEM((2, 1536, 1024), BF16),
            pltpu.VMEM((1440, 1440), BF16),
            pltpu.VMEM((1440, 1440), BF16),
            pltpu.VMEM((3, 4, 768, 768), BF16),
            pltpu.VMEM((3, 4, 3, 192, 768), BF16),
            pltpu.VMEM((3, 4, 3, 48, 768), BF16),
            pltpu.VMEM((4, 1456, 128), BF16),
            pltpu.VMEM((2, 3, 736, 128), BF16),
            pltpu.VMEM((768, 720), BF16),
            pltpu.VMEM((1, 1024), F32),
            pltpu.SemaphoreType.DMA((6,)),
            pltpu.SemaphoreType.DMA((2, 8, 2)),
            pltpu.SemaphoreType.DMA((2, 8, 2)),
            pltpu.SemaphoreType.DMA((3, 4, 6)),
            pltpu.SemaphoreType.DMA((3, 4, 6)),
            pltpu.SemaphoreType.DMA,
            pltpu.SemaphoreType.DMA,
            pltpu.SemaphoreType.DMA((2, 3)),
            pltpu.SemaphoreType.DMA((2, 3)),
        ],
        compiler_params=pltpu.CompilerParams(
            collective_id=0, has_side_effects=True, vmem_limit_bytes=64 * 1024 * 1024
        ),
    )(x, og, ids, probs, wg, wu, wd)


def on_device(tokens, out_grad, expert_ids, probs, w_gate, w_up, w_down):
    out, ig, routed = layer(
        tokens.T, out_grad.T, expert_ids.T, probs.T, w_gate[0], w_up[0], w_down[0]
    )
    down, gate, up = [jnp.transpose(out[m], (1, 0, 2)) for m in range(3)]
    return ig.T, routed.T, gate, up, down


def solution(mesh):
    tok = P(("dp", "expert"), None)
    w = P("expert", None, None)
    g = P("expert", "dp", None)
    return jax.shard_map(
        on_device,
        mesh=mesh,
        in_specs=(tok, tok, tok, tok, w, w, w),
        out_specs=(tok, tok, g, g, g),
        check_vma=False,
    )
```

```python
import functools

import jax
import jax.numpy as jnp
from jax import lax
from jax.experimental import pallas as pl
from jax.experimental.pallas import tpu as pltpu
from jax.sharding import PartitionSpec as P

BF16, F32 = jnp.bfloat16, jnp.float32
MESH = pl.DeviceIdType.MESH
NT = (((1,), (1,)), ((), ()))
NN = (((1,), (0,)), ((), ()))
CHIP = 256


def mod4(v):
    return lax.rem(v + 8, 4)


def place():
    dp = lax.axis_index("dp")
    ex = lax.axis_index("expert")
    return dp // 4, lax.rem(dp, 4), ex // 2, lax.rem(ex, 2)


def kernel(
    x_h, og_h, ids, probs, wg_h, wu_h, wd_h,
    out, ig_out, routed,
    xg, og, xp, hp, gu, wa, wb, terms, r1, r2, sib, rx, spread, racc,
    load, g_send, g_recv, s_send, s_recv, b_send, b_recv, x_send, x_recv,
):
    y, z, x, c = place()
    dp, ex = y * 4 + z, x * 2 + c

    def at(dp_to=None, ex_to=None):
        return (dp if dp_to is None else dp_to, ex if ex_to is None else ex_to)

    def along(axis, d):
        if axis == "y":
            return at(dp_to=mod4(y + d) * 4 + z)
        if axis == "z":
            return at(dp_to=y * 4 + mod4(z + d))
        return at(ex_to=mod4(x + d) * 2 + c)


    own_x = pltpu.make_async_copy(x_h, xg.at[x, c, 0:1440], load.at[0])
    own_og = pltpu.make_async_copy(og_h, og.at[x, c, 0:1440], load.at[1])
    load_g = pltpu.make_async_copy(wg_h, wa, load.at[2])
    load_u = pltpu.make_async_copy(wu_h, wb, load.at[3])
    load_d = pltpu.make_async_copy(wd_h, wa, load.at[4])
    load_g2 = pltpu.make_async_copy(wg_h, wa, load.at[5])
    for copy in (own_x, own_og, load_g, load_u):
        copy.start()
    sibling = at(ex_to=x * 2 + 1 - c)
    barrier = pltpu.get_barrier_semaphore()
    for to in [along(a, d) for a in "xyz" for d in (1, -1)] + [sibling]:
        pl.semaphore_signal(barrier, inc=1, device_id=to, device_id_type=MESH)

    left, right, far = mod4(x - 1), mod4(x + 1), mod4(x + 2)

    def hop(a, kind, half, got=False):
        buf = (xg, og)[a]
        rows = slice(0, 768) if half == 0 else slice(768, 1456 if a == 0 else 1440)
        n, sent, arrived, to = {
            "right": (0, x, left, along("x", 1)),
            "left": (1, x, right, along("x", -1)),
            "pass_right": (2, left, far, along("x", 1)),
            "pass_left": (3, right, far, along("x", -1)),
            "core_own": (4, x, x, sibling),
            "core_left": (5, left, left, sibling),
            "core_right": (6, right, right, sibling),
            "core_far": (7, far, far, sibling),
        }[kind]
        core = 1 - c if got and n >= 4 else c
        block = buf.at[arrived if got else sent, core, rows]
        return pltpu.make_async_remote_copy(
            src_ref=block, dst_ref=block, send_sem=g_send.at[a, n, half],
            recv_sem=g_recv.at[a, n, half], device_id=to, device_id_type=MESH,
        )

    sent = []

    def send(a, *names):
        for name, half in names:
            hop(a, name, half).start()
            sent.append((a, name, half))

    def got(a, *names):
        for name, half in names:
            hop(a, name, half, got=True).wait_recv()

    def both(name):
        return (name, 0), (name, 1)

    rowid = lax.broadcasted_iota(jnp.int32, (16, 128), 0)
    dense = jnp.zeros((16, 128), F32)
    for k in range(4):
        dense = dense + jnp.where(ids[k : k + 1, :] == rowid, probs[k : k + 1, :].astype(F32), 0.0)
    xg[x, c, 1440:1456, :] = dense.astype(BF16)
    own_x.wait()
    pl.semaphore_wait(barrier, 7)
    send(0, ("right", 0), ("left", 1), *both("core_own"))

    row = lax.broadcasted_iota(jnp.int32, (768, 720), 0)
    col = lax.broadcasted_iota(jnp.int32, (768, 720), 1)
    rest = row - 384
    above = lax.div(row, 192) * 360 + lax.div(lax.rem(row, 192), 48) * 90 + lax.rem(row, 48)
    below = lax.rem(lax.div(rest, 48), 2) * 360 + lax.div(rest, 96) * 90 + 48 + lax.rem(rest, 48)
    kept = lax.rem(row, 48) < 42
    picked = ((row < 384) & (above == col)) | ((row >= 384) & kept & (below == col))
    spread[...] = jnp.where(picked, 1.0, 0.0).astype(BF16)

    def flip(w, m):
        for k in range(4):
            n = 384 if k < 3 else 288
            t = w[:, k * 384 : k * 384 + n].T
            for h in range(2):
                r0, r1_ = max(k * 384, h * 720), min(k * 384 + n, h * 720 + 720)
                if r0 < r1_:
                    part = t[r0 - k * 384 : r1_ - k * 384]
                    to = slice(r0 - h * 720, r1_ - h * 720)
                    terms[m, 2 * h, to, :] = part[:, 0:768]
                    terms[m, 2 * h + 1, to, 0:672] = part[:, 768:1440]

    def lanes_of(chip):
        return pl.ds(pl.multiple_of(chip * CHIP, CHIP), CHIP)

    def gate_of(chip):
        parts = []
        for k in range(2):
            rows = xg[chip, k, 1440:1456, :].astype(F32)
            parts.append(jnp.sum(jnp.where(rowid == ex, rows, 0.0), axis=0, keepdims=True))
        return jnp.concatenate(parts, axis=1)

    def place_rows(to, h, v, lanes):
        t = lax.dot_general(spread[...], v, NN, preferred_element_type=F32).astype(BF16)
        to[h * 384 : h * 384 + 384, lanes] = t[0:384]
        for k in range(4):
            r0 = 768 + k * 192 + h * 96
            to[r0 : r0 + 96, lanes] = t[384 + k * 96 : 480 + k * 96]

    def forward(chip):
        lanes = lanes_of(chip)
        gate = gate_of(chip)
        cols = jnp.concatenate([xg[chip, 0, 0:1440, :], xg[chip, 1, 0:1440, :]], axis=1)
        for h in range(2):
            rows = slice(h * 720, h * 720 + 720)
            g, u = [
                lax.dot_general(
                    terms[m, 2 * h, 0:720, :], cols[0:768], NN, preferred_element_type=F32
                )
                + lax.dot_general(
                    terms[m, 2 * h + 1, 0:720, 0:672], cols[768:1440], NN, preferred_element_type=F32
                )
                for m in range(2)
            ]
            s = 0.5 * jnp.tanh(0.5 * g) + 0.5
            gs = g * s
            hidden = gs * u
            gu[0, rows, lanes] = (u * (s + gs * (1.0 - s))).astype(BF16)
            gu[1, rows, lanes] = gs.astype(BF16)
            xp[rows, lanes] = hidden.astype(BF16)
            place_rows(hp, h, (gate * hidden).astype(BF16), lanes)

    def gradient(chip):
        lanes = lanes_of(chip)
        gate = gate_of(chip)
        cols = jnp.concatenate([og[chip, 0, 0:1440, :], og[chip, 1, 0:1440, :]], axis=1)
        total = jnp.zeros((1, CHIP), F32)
        for h in range(2):
            rows = slice(h * 720, h * 720 + 720)
            a = lax.dot_general(wa[rows, :], cols, NN, preferred_element_type=F32)
            pa = gate * a
            gu[0, rows, lanes] = (pa * gu[0, rows, lanes].astype(F32)).astype(BF16)
            gu[1, rows, lanes] = (pa * gu[1, rows, lanes].astype(F32)).astype(BF16)
            hidden = xp[rows, lanes].astype(F32)
            total = total + jnp.sum(hidden * a, axis=0, keepdims=True)
        racc[:, lanes] = total

    def widen(chip):
        for h in range(2):
            rows = slice(h * 720, h * 720 + 720)
            v = jnp.concatenate([xg[chip, 0, rows, :], xg[chip, 1, rows, :]], axis=1)
            place_rows(xp, h, v, lanes_of(chip))

    def way(s):
        first = 1 - s // 2
        d = 1 - 2 * lax.rem(s, 2)
        return first, d

    def step_to(on_y, d):
        return at(dp_to=mod4(y + d * on_y) * 4 + mod4(z + d * (1 - on_y)))

    def chunk(index):
        return pl.ds(pl.multiple_of(index * 192, 64), 192)

    def share(index):
        return pl.ds(pl.multiple_of(index * 48, 16), 48)

    def first_copy(m, s, t):
        on_y, d = way(s)
        pos = y * on_y + z * (1 - on_y)
        go = -d if t == 1 else d
        src = r1.at[m, s, 0] if t == 2 else terms.at[m, s, chunk(mod4(pos + (2 * d, -d)[t]))]
        return pltpu.make_async_remote_copy(
            src_ref=src, dst_ref=r1.at[m, s, t], send_sem=s_send.at[m, s, t],
            recv_sem=s_recv.at[m, s, t], device_id=step_to(on_y, go), device_id_type=MESH,
        )

    def second_copy(m, s, t):
        on_y, d = way(s)
        pos = z * on_y + y * (1 - on_y)
        go = -d if t == 1 else d
        src = r2.at[m, s, 0] if t == 2 else r1.at[m, s, 2, share(mod4(pos + (2 * d, -d)[t]))]
        return pltpu.make_async_remote_copy(
            src_ref=src, dst_ref=r2.at[m, s, t], send_sem=s_send.at[m, s, 3 + t],
            recv_sem=s_recv.at[m, s, 3 + t], device_id=step_to(1 - on_y, go), device_id_type=MESH,
        )

    def start(m):
        def body(s, carry):
            r0 = pl.multiple_of((s // 2) * 768, 768)
            c0 = pl.multiple_of(lax.rem(s, 2) * 768, 768)
            a = (hp if m == 0 else xp)[pl.ds(r0, 768), :]
            if m == 0:
                parts = [og[k // 2, k % 2, pl.ds(c0, 768), :] for k in range(8)]
                b = jnp.concatenate(parts, axis=1)
            else:
                b = gu[m - 1, pl.ds(c0, 768), :]
            terms[m, s] = lax.dot_general(a, b, NT, preferred_element_type=F32).astype(BF16)
            first_copy(m, s, 0).start()
            first_copy(m, s, 1).start()
            return carry

        lax.fori_loop(0, 4, body, 0)

    def advance(m, stage):
        def body(s, carry):
            on_y, d = way(s)
            if stage < 2:
                pos = y * on_y + z * (1 - on_y)
                if stage == 0:
                    first_copy(m, s, 0).wait_recv()
                    r1[m, s, 0] = r1[m, s, 0] + terms[m, s, chunk(mod4(pos + d)), :]
                    first_copy(m, s, 2).start()
                else:
                    first_copy(m, s, 1).wait_recv()
                    first_copy(m, s, 2).wait_recv()
                    mine = terms[m, s, chunk(pos), :].astype(F32) + r1[m, s, 1].astype(F32)
                    r1[m, s, 2] = (r1[m, s, 2].astype(F32) + mine).astype(BF16)
                    second_copy(m, s, 0).start()
                    second_copy(m, s, 1).start()
                return carry
            pos = z * on_y + y * (1 - on_y)
            if stage == 2:
                second_copy(m, s, 0).wait_recv()
                r2[m, s, 0] = r2[m, s, 0] + r1[m, s, 2, share(mod4(pos + d)), :]
                second_copy(m, s, 2).start()
            else:
                second_copy(m, s, 1).wait_recv()
                second_copy(m, s, 2).wait_recv()
                mine = r1[m, s, 2, share(pos), :].astype(F32)
                total = r2[m, s, 1].astype(F32) + r2[m, s, 2].astype(F32) + mine
                r0, n = 48 * (s // 2), 48 - 6 * (s // 2)
                lanes = (s % 2) * 768
                width = 768 - 96 * (s % 2)
                out[m, r0 : r0 + n, 0, lanes : lanes + width] = total[0:n, 0:width]
            return carry

        if stage < 3:
            lax.fori_loop(0, 4, body, 0)
        else:
            for s in range(4):
                body(s, 0)

    def ig_chip(chip):
        lanes = slice(chip * CHIP, chip * CHIP + CHIP)

        def body(h, carry):
            rows = pl.ds(pl.multiple_of(h * 720, 16), 720)
            t = lax.dot_general(wa[rows, :], gu[0, 0:1440, lanes], NN, preferred_element_type=F32)
            u = lax.dot_general(wb[rows, :], gu[1, 0:1440, lanes], NN, preferred_element_type=F32)
            t = (t + u).astype(BF16)
            xg[chip, 0, rows, :] = t[:, 0:128]
            xg[chip, 1, rows, :] = t[:, 128:256]
            return carry

        lax.fori_loop(0, 2, body, 0)

    sib_copy = pltpu.make_async_remote_copy(
        src_ref=xg.at[:, 1 - c], dst_ref=sib, send_sem=b_send, recv_sem=b_recv,
        device_id=sibling, device_id_type=MESH,
    )
    halves = ((1, 0, 720), (-1, 720, 736))

    def x_copy(h, t):
        d, lo, n = halves[h]
        src = sib.at[mod4(x - d), lo : lo + n] if t == 0 else rx.at[h, t - 1, 0:n]
        return pltpu.make_async_remote_copy(
            src_ref=src, dst_ref=rx.at[h, t, 0:n], send_sem=x_send.at[h, t],
            recv_sem=x_recv.at[h, t], device_id=along("x", d), device_id_type=MESH,
        )

    def ig_pair():
        sib_copy.wait_recv()
        for k in range(4):
            sib[k] = sib[k] + xg[k, c]
        for h in range(2):
            x_copy(h, 0).start()

    def ig_step(t):
        for h in range(2):
            d, lo, n = halves[h]
            x_copy(h, t).wait_recv()
            own = sib[mod4(x - d * (2 + t)), lo : lo + n]
            if t < 2:
                rx[h, t, 0:n] = rx[h, t, 0:n] + own
                x_copy(h, t + 1).start()
            else:
                total = rx[h, t, 0:n].astype(F32) + own.astype(F32)
                ig_out[lo : lo + 720, :] = total[0:720].astype(BF16)
                if h == 1:
                    for k in range(4):
                        mine = jnp.where(ids[k : k + 1, :] == rowid, total[720:736], 0.0)
                        routed[k : k + 1, :] = jnp.sum(mine, axis=0, keepdims=True).astype(BF16)

    load_g.wait()
    flip(wa, 0)
    load_d.start()
    load_u.wait()
    flip(wb, 1)
    hop(0, "right", 0).wait_send()
    sent.remove((0, "right", 0))
    send(0, ("right", 1))
    hop(0, "left", 1).wait_send()
    sent.remove((0, "left", 1))
    send(0, ("left", 0))

    def chip_at(i):
        return mod4(x + i + (i // 2) * (1 - 2 * lax.rem(i, 2)))

    def forwards(i, carry):
        @pl.when(i == 0)
        def _():
            got(0, *both("core_own"))

        @pl.when(i == 1)
        def _():
            got(0, ("right", 0))
            send(0, ("pass_right", 0))
            got(0, ("left", 1))
            send(0, ("pass_left", 1))
            own_og.wait()
            send(1, *both("right"), *both("left"), *both("core_own"))
            got(0, ("left", 0))
            send(0, *both("core_right"))
            got(0, ("right", 1))
            send(0, *both("core_left"))
            got(0, *both("core_right"))

        @pl.when(i == 2)
        def _():
            got(0, *both("core_left"))

        @pl.when(i == 3)
        def _():
            got(0, ("pass_right", 0), ("pass_left", 1))
            send(0, *both("core_far"))
            got(0, *both("core_far"))

        forward(chip_at(i))
        return carry

    def widens(i, carry):
        widen(chip_at(i))
        return carry

    def gradients(i, carry):
        @pl.when(i == 0)
        def _():
            load_d.wait()
            got(1, *both("core_own"))

        @pl.when(i == 1)
        def _():
            got(1, ("right", 0))
            send(1, ("pass_right", 0))
            got(1, ("left", 1))
            send(1, ("pass_left", 1))
            got(1, ("left", 0))
            send(1, *both("core_right"))
            got(1, ("right", 1))
            send(1, *both("core_left"))
            got(1, *both("core_right"))

        @pl.when(i == 2)
        def _():
            got(1, *both("core_left"))

        @pl.when(i == 3)
        def _():
            got(1, ("pass_right", 0), ("pass_left", 1))
            send(1, *both("core_far"))
            lax.fori_loop(0, 3, widens, 0)
            got(1, *both("core_far"))
            start(0)

        gradient(chip_at(i))
        return carry

    lax.fori_loop(0, 4, forwards, 0)
    lax.fori_loop(0, 4, gradients, 0)
    load_g2.start()
    lax.fori_loop(3, 4, widens, 0)
    start(1)
    start(2)
    for a, name, half in sent:
        if a == 0:
            hop(a, name, half).wait_send()
    for b in range(8):
        part = jnp.broadcast_to(racc[:, b * 128 : (b + 1) * 128], (16, 128))
        xg[b // 2, b % 2, 1440:1456, :] = jnp.where(rowid == ex, part, 0.0).astype(BF16)
    load_g2.wait()
    ig_chip(0)
    ig_chip(1)
    advance(0, 0)
    ig_chip(2)
    ig_chip(3)
    sib_copy.start()
    advance(1, 0)
    advance(2, 0)
    ig_pair()
    advance(0, 1)
    ig_step(0)
    advance(0, 2)
    advance(1, 1)
    advance(2, 1)
    ig_step(1)
    advance(0, 3)
    advance(1, 2)
    advance(2, 2)
    ig_step(2)
    advance(1, 3)
    advance(2, 3)
    sib_copy.wait_send()
    for h in range(2):
        for t in range(3):
            x_copy(h, t).wait_send()
    for m in range(3):
        for s in range(4):
            for t in range(3):
                first_copy(m, s, t).wait_send()
                second_copy(m, s, t).wait_send()
    for a, name, half in sent:
        if a == 1:
            hop(a, name, half).wait_send()


def layer(x, og, ids, probs, wg, wu, wd):
    hbm = pl.BlockSpec(memory_space=pl.ANY)
    vmem = pl.BlockSpec(memory_space=pltpu.VMEM)
    return pl.pallas_call(
        kernel,
        out_shape=(
            jax.ShapeDtypeStruct((3, 90, 1, 1440), F32),
            jax.ShapeDtypeStruct((1440, 128), BF16),
            jax.ShapeDtypeStruct((4, 128), BF16),
        ),
        in_specs=[hbm, hbm, vmem, vmem, hbm, hbm, hbm],
        out_specs=(vmem,) * 3,
        scratch_shapes=[
            pltpu.VMEM((4, 2, 1456, 128), BF16),
            pltpu.VMEM((4, 2, 1536, 128), BF16),
            pltpu.VMEM((1536, 1024), BF16),
            pltpu.VMEM((1536, 1024), BF16),
            pltpu.VMEM((2, 1536, 1024), BF16),
            pltpu.VMEM((1440, 1440), BF16),
            pltpu.VMEM((1440, 1440), BF16),
            pltpu.VMEM((3, 4, 768, 768), BF16),
            pltpu.VMEM((3, 4, 3, 192, 768), BF16),
            pltpu.VMEM((3, 4, 3, 48, 768), BF16),
            pltpu.VMEM((4, 1456, 128), BF16),
            pltpu.VMEM((2, 3, 736, 128), BF16),
            pltpu.VMEM((768, 720), BF16),
            pltpu.VMEM((1, 1024), F32),
            pltpu.SemaphoreType.DMA((6,)),
            pltpu.SemaphoreType.DMA((2, 8, 2)),
            pltpu.SemaphoreType.DMA((2, 8, 2)),
            pltpu.SemaphoreType.DMA((3, 4, 6)),
            pltpu.SemaphoreType.DMA((3, 4, 6)),
            pltpu.SemaphoreType.DMA,
            pltpu.SemaphoreType.DMA,
            pltpu.SemaphoreType.DMA((2, 3)),
            pltpu.SemaphoreType.DMA((2, 3)),
        ],
        compiler_params=pltpu.CompilerParams(
            collective_id=0, has_side_effects=True, vmem_limit_bytes=64 * 1024 * 1024
        ),
    )(x, og, ids, probs, wg, wu, wd)


def on_device(tokens, out_grad, expert_ids, probs, w_gate, w_up, w_down):
    out, ig, routed = layer(
        tokens.T, out_grad.T, expert_ids.T, probs.T, w_gate[0], w_up[0], w_down[0]
    )
    down, gate, up = [jnp.transpose(out[m], (1, 0, 2)) for m in range(3)]
    return ig.T, routed.T, gate, up, down


def solution(mesh):
    tok = P(("dp", "expert"), None)
    w = P("expert", None, None)
    g = P("expert", "dp", None)
    return jax.shard_map(
        on_device,
        mesh=mesh,
        in_specs=(tok, tok, tok, tok, w, w, w),
        out_specs=(tok, tok, g, g, g),
        check_vma=False,
    )
```

```python
import functools

import jax
import jax.numpy as jnp
from jax import lax
from jax.experimental import pallas as pl
from jax.experimental.pallas import tpu as pltpu
from jax.sharding import PartitionSpec as P

BF16, F32 = jnp.bfloat16, jnp.float32
MESH = pl.DeviceIdType.MESH
NT = (((1,), (1,)), ((), ()))
NN = (((1,), (0,)), ((), ()))
CHIP = 256


def mod4(v):
    return lax.rem(v + 8, 4)


def place():
    dp = lax.axis_index("dp")
    ex = lax.axis_index("expert")
    return dp // 4, lax.rem(dp, 4), ex // 2, lax.rem(ex, 2)


def kernel(
    x_h, og_h, ids, probs, wg_h, wu_h, wd_h,
    out, ig_out, routed,
    xg, og, xp, hp, gu, wa, wb, terms, r1, r2, sib, rx, spread, racc,
    load, g_send, g_recv, s_send, s_recv, b_send, b_recv, x_send, x_recv,
):
    y, z, x, c = place()
    dp, ex = y * 4 + z, x * 2 + c

    def at(dp_to=None, ex_to=None):
        return (dp if dp_to is None else dp_to, ex if ex_to is None else ex_to)

    def along(axis, d):
        if axis == "y":
            return at(dp_to=mod4(y + d) * 4 + z)
        if axis == "z":
            return at(dp_to=y * 4 + mod4(z + d))
        return at(ex_to=mod4(x + d) * 2 + c)


    own_x = pltpu.make_async_copy(x_h, xg.at[x, c, 0:1440], load.at[0])
    own_og = pltpu.make_async_copy(og_h, og.at[x, c, 0:1440], load.at[1])
    load_g = pltpu.make_async_copy(wg_h, wa, load.at[2])
    load_u = pltpu.make_async_copy(wu_h, wb, load.at[3])
    load_d = pltpu.make_async_copy(wd_h, wa, load.at[4])
    load_g2 = pltpu.make_async_copy(wg_h, wa, load.at[5])
    own_x.start()
    sibling = at(ex_to=x * 2 + 1 - c)
    barrier = pltpu.get_barrier_semaphore()
    for to in [along(a, d) for a in "xyz" for d in (1, -1)] + [sibling]:
        pl.semaphore_signal(barrier, inc=1, device_id=to, device_id_type=MESH)

    left, right, far = mod4(x - 1), mod4(x + 1), mod4(x + 2)

    def hop(a, kind, half, got=False):
        buf = (xg, og)[a]
        rows = slice(0, 768) if half == 0 else slice(768, 1456 if a == 0 else 1440)
        n, sent, arrived, to = {
            "right": (0, x, left, along("x", 1)),
            "left": (1, x, right, along("x", -1)),
            "pass_right": (2, left, far, along("x", 1)),
            "pass_left": (3, right, far, along("x", -1)),
            "core_own": (4, x, x, sibling),
            "core_left": (5, left, left, sibling),
            "core_right": (6, right, right, sibling),
            "core_far": (7, far, far, sibling),
        }[kind]
        core = 1 - c if got and n >= 4 else c
        block = buf.at[arrived if got else sent, core, rows]
        return pltpu.make_async_remote_copy(
            src_ref=block, dst_ref=block, send_sem=g_send.at[a, n, half],
            recv_sem=g_recv.at[a, n, half], device_id=to, device_id_type=MESH,
        )

    sent = []

    def send(a, *names):
        for name, half in names:
            hop(a, name, half).start()
            sent.append((a, name, half))

    def got(a, *names):
        for name, half in names:
            hop(a, name, half, got=True).wait_recv()

    def both(name):
        return (name, 0), (name, 1)

    rowid = lax.broadcasted_iota(jnp.int32, (16, 128), 0)
    dense = jnp.zeros((16, 128), F32)
    for k in range(4):
        dense = dense + jnp.where(ids[k : k + 1, :] == rowid, probs[k : k + 1, :].astype(F32), 0.0)
    xg[x, c, 1440:1456, :] = dense.astype(BF16)
    own_x.wait()
    for copy in (load_g, load_u, own_og):
        copy.start()
    row = lax.broadcasted_iota(jnp.int32, (768, 1), 0)
    rest = row - 384
    above = lax.div(row, 192) * 360 + lax.div(lax.rem(row, 192), 48) * 90 + lax.rem(row, 48)
    below = lax.rem(lax.div(rest, 48), 2) * 360 + lax.div(rest, 96) * 90 + 48 + lax.rem(rest, 48)
    below = jnp.where(lax.rem(row, 48) < 42, below, -1)
    source = jnp.where(row < 384, above, below)
    picked = source == lax.broadcasted_iota(jnp.int32, (768, 720), 1)
    spread[...] = jnp.where(picked, 1.0, 0.0).astype(BF16)
    pl.semaphore_wait(barrier, 7)
    send(0, ("right", 0), ("left", 1), *both("core_own"))

    def flip(w, m):
        for k in range(4):
            n = 384 if k < 3 else 288
            t = w[:, k * 384 : k * 384 + n].T
            for h in range(2):
                r0, r1_ = max(k * 384, h * 720), min(k * 384 + n, h * 720 + 720)
                if r0 < r1_:
                    part = t[r0 - k * 384 : r1_ - k * 384]
                    to = slice(r0 - h * 720, r1_ - h * 720)
                    terms[m, 2 * h, to, :] = part[:, 0:768]
                    terms[m, 2 * h + 1, to, 0:672] = part[:, 768:1440]

    def lanes_of(chip):
        return pl.ds(pl.multiple_of(chip * CHIP, CHIP), CHIP)

    def gate_of(chip):
        parts = []
        for k in range(2):
            rows = xg[chip, k, 1440:1456, :].astype(F32)
            parts.append(jnp.sum(jnp.where(rowid == ex, rows, 0.0), axis=0, keepdims=True))
        return jnp.concatenate(parts, axis=1)

    def place_rows(to, h, v, lanes):
        t = lax.dot_general(spread[...], v, NN, preferred_element_type=F32).astype(BF16)
        to[h * 384 : h * 384 + 384, lanes] = t[0:384]
        for k in range(4):
            r0 = 768 + k * 192 + h * 96
            to[r0 : r0 + 96, lanes] = t[384 + k * 96 : 480 + k * 96]

    def forward(chip):
        lanes = lanes_of(chip)
        gate = gate_of(chip)
        cols = jnp.concatenate([xg[chip, 0, 0:1440, :], xg[chip, 1, 0:1440, :]], axis=1)
        for h in range(2):
            rows = slice(h * 720, h * 720 + 720)
            g, u = [
                lax.dot_general(
                    terms[m, 2 * h, 0:720, :], cols[0:768], NN, preferred_element_type=F32
                )
                + lax.dot_general(
                    terms[m, 2 * h + 1, 0:720, 0:672], cols[768:1440], NN, preferred_element_type=F32
                )
                for m in range(2)
            ]
            s = 0.5 * jnp.tanh(0.5 * g) + 0.5
            gs = g * s
            hidden = gs * u
            gu[0, rows, lanes] = (u * (s + gs * (1.0 - s))).astype(BF16)
            gu[1, rows, lanes] = gs.astype(BF16)
            xp[rows, lanes] = hidden.astype(BF16)
            place_rows(hp, h, (gate * hidden).astype(BF16), lanes)

    def gradient(chip):
        lanes = lanes_of(chip)
        gate = gate_of(chip)
        cols = jnp.concatenate([og[chip, 0, 0:1440, :], og[chip, 1, 0:1440, :]], axis=1)
        total = jnp.zeros((1, CHIP), F32)
        for h in range(2):
            rows = slice(h * 720, h * 720 + 720)
            a = lax.dot_general(wa[rows, :], cols, NN, preferred_element_type=F32)
            pa = gate * a
            gu[0, rows, lanes] = (pa * gu[0, rows, lanes].astype(F32)).astype(BF16)
            gu[1, rows, lanes] = (pa * gu[1, rows, lanes].astype(F32)).astype(BF16)
            hidden = xp[rows, lanes].astype(F32)
            total = total + jnp.sum(hidden * a, axis=0, keepdims=True)
        racc[:, lanes] = total

    def widen(chip):
        for h in range(2):
            rows = slice(h * 720, h * 720 + 720)
            v = jnp.concatenate([xg[chip, 0, rows, :], xg[chip, 1, rows, :]], axis=1)
            place_rows(xp, h, v, lanes_of(chip))

    def way(s):
        first = 1 - s // 2
        d = 1 - 2 * lax.rem(s, 2)
        return first, d

    def step_to(on_y, d):
        return at(dp_to=mod4(y + d * on_y) * 4 + mod4(z + d * (1 - on_y)))

    def chunk(index):
        return pl.ds(pl.multiple_of(index * 192, 64), 192)

    def share(index):
        return pl.ds(pl.multiple_of(index * 48, 16), 48)

    def first_copy(m, s, t):
        on_y, d = way(s)
        pos = y * on_y + z * (1 - on_y)
        go = -d if t == 1 else d
        src = r1.at[m, s, 0] if t == 2 else terms.at[m, s, chunk(mod4(pos + (2 * d, -d)[t]))]
        return pltpu.make_async_remote_copy(
            src_ref=src, dst_ref=r1.at[m, s, t], send_sem=s_send.at[m, s, t],
            recv_sem=s_recv.at[m, s, t], device_id=step_to(on_y, go), device_id_type=MESH,
        )

    def second_copy(m, s, t):
        on_y, d = way(s)
        pos = z * on_y + y * (1 - on_y)
        go = -d if t == 1 else d
        src = r2.at[m, s, 0] if t == 2 else r1.at[m, s, 2, share(mod4(pos + (2 * d, -d)[t]))]
        return pltpu.make_async_remote_copy(
            src_ref=src, dst_ref=r2.at[m, s, t], send_sem=s_send.at[m, s, 3 + t],
            recv_sem=s_recv.at[m, s, 3 + t], device_id=step_to(1 - on_y, go), device_id_type=MESH,
        )

    def start(m):
        def body(s, carry):
            r0 = pl.multiple_of((s // 2) * 768, 768)
            c0 = pl.multiple_of(lax.rem(s, 2) * 768, 768)
            a = (hp if m == 0 else xp)[pl.ds(r0, 768), :]
            if m == 0:
                parts = [og[k // 2, k % 2, pl.ds(c0, 768), :] for k in range(8)]
                b = jnp.concatenate(parts, axis=1)
            else:
                b = gu[m - 1, pl.ds(c0, 768), :]
            terms[m, s] = lax.dot_general(a, b, NT, preferred_element_type=F32).astype(BF16)
            first_copy(m, s, 0).start()
            first_copy(m, s, 1).start()
            return carry

        lax.fori_loop(0, 4, body, 0)

    def advance(m, stage):
        def body(s, carry):
            on_y, d = way(s)
            if stage < 2:
                pos = y * on_y + z * (1 - on_y)
                if stage == 0:
                    first_copy(m, s, 0).wait_recv()
                    r1[m, s, 0] = r1[m, s, 0] + terms[m, s, chunk(mod4(pos + d)), :]
                    first_copy(m, s, 2).start()
                else:
                    first_copy(m, s, 1).wait_recv()
                    first_copy(m, s, 2).wait_recv()
                    mine = terms[m, s, chunk(pos), :].astype(F32) + r1[m, s, 1].astype(F32)
                    r1[m, s, 2] = (r1[m, s, 2].astype(F32) + mine).astype(BF16)
                    second_copy(m, s, 0).start()
                    second_copy(m, s, 1).start()
                return carry
            pos = z * on_y + y * (1 - on_y)
            if stage == 2:
                second_copy(m, s, 0).wait_recv()
                r2[m, s, 0] = r2[m, s, 0] + r1[m, s, 2, share(mod4(pos + d)), :]
                second_copy(m, s, 2).start()
            else:
                second_copy(m, s, 1).wait_recv()
                second_copy(m, s, 2).wait_recv()
                mine = r1[m, s, 2, share(pos), :].astype(F32)
                total = r2[m, s, 1].astype(F32) + r2[m, s, 2].astype(F32) + mine
                r0, n = 48 * (s // 2), 48 - 6 * (s // 2)
                lanes = (s % 2) * 768
                width = 768 - 96 * (s % 2)
                out[m, r0 : r0 + n, 0, lanes : lanes + width] = total[0:n, 0:width]
            return carry

        if stage < 3:
            lax.fori_loop(0, 4, body, 0)
        else:
            for s in range(4):
                body(s, 0)

    def ig_chip(chip):
        lanes = slice(chip * CHIP, chip * CHIP + CHIP)

        def body(h, carry):
            rows = pl.ds(pl.multiple_of(h * 720, 16), 720)
            t = lax.dot_general(wa[rows, :], gu[0, 0:1440, lanes], NN, preferred_element_type=F32)
            u = lax.dot_general(wb[rows, :], gu[1, 0:1440, lanes], NN, preferred_element_type=F32)
            t = (t + u).astype(BF16)
            xg[chip, 0, rows, :] = t[:, 0:128]
            xg[chip, 1, rows, :] = t[:, 128:256]
            return carry

        lax.fori_loop(0, 2, body, 0)

    sib_copy = pltpu.make_async_remote_copy(
        src_ref=xg.at[:, 1 - c], dst_ref=sib, send_sem=b_send, recv_sem=b_recv,
        device_id=sibling, device_id_type=MESH,
    )
    halves = ((1, 0, 720), (-1, 720, 736))

    def x_copy(h, t):
        d, lo, n = halves[h]
        src = sib.at[mod4(x - d), lo : lo + n] if t == 0 else rx.at[h, t - 1, 0:n]
        return pltpu.make_async_remote_copy(
            src_ref=src, dst_ref=rx.at[h, t, 0:n], send_sem=x_send.at[h, t],
            recv_sem=x_recv.at[h, t], device_id=along("x", d), device_id_type=MESH,
        )

    def ig_pair():
        sib_copy.wait_recv()
        for k in range(4):
            sib[k] = sib[k] + xg[k, c]
        for h in range(2):
            x_copy(h, 0).start()

    def ig_step(t):
        for h in range(2):
            d, lo, n = halves[h]
            x_copy(h, t).wait_recv()
            own = sib[mod4(x - d * (2 + t)), lo : lo + n]
            if t < 2:
                rx[h, t, 0:n] = rx[h, t, 0:n] + own
                x_copy(h, t + 1).start()
            else:
                total = rx[h, t, 0:n].astype(F32) + own.astype(F32)
                ig_out[lo : lo + 720, :] = total[0:720].astype(BF16)
                if h == 1:
                    for k in range(4):
                        mine = jnp.where(ids[k : k + 1, :] == rowid, total[720:736], 0.0)
                        routed[k : k + 1, :] = jnp.sum(mine, axis=0, keepdims=True).astype(BF16)

    load_g.wait()
    flip(wa, 0)
    load_d.start()
    load_u.wait()
    flip(wb, 1)
    hop(0, "right", 0).wait_send()
    sent.remove((0, "right", 0))
    send(0, ("right", 1))
    hop(0, "left", 1).wait_send()
    sent.remove((0, "left", 1))
    send(0, ("left", 0))

    def chip_at(i):
        return mod4(x + i + (i // 2) * (1 - 2 * lax.rem(i, 2)))

    def forwards(i, carry):
        @pl.when(i == 0)
        def _():
            got(0, *both("core_own"))

        @pl.when(i == 1)
        def _():
            got(0, ("right", 0))
            send(0, ("pass_right", 0))
            got(0, ("left", 1))
            send(0, ("pass_left", 1))
            own_og.wait()
            send(1, ("right", 0), ("left", 1), *both("core_own"))
            got(0, ("left", 0))
            send(0, *both("core_right"))
            got(0, ("right", 1))
            send(0, *both("core_left"))
            got(0, *both("core_right"))

        @pl.when(i == 2)
        def _():
            send(1, ("right", 1), ("left", 0))
            got(0, *both("core_left"))

        @pl.when(i == 3)
        def _():
            got(0, ("pass_right", 0), ("pass_left", 1))
            send(0, *both("core_far"))
            got(1, ("right", 0))
            send(1, ("pass_right", 0))
            got(1, ("left", 1))
            send(1, ("pass_left", 1))
            got(0, *both("core_far"))

        forward(chip_at(i))
        return carry

    def widens(i, carry):
        widen(chip_at(i))
        return carry

    def gradients(i, carry):
        @pl.when(i == 0)
        def _():
            load_d.wait()
            got(1, *both("core_own"))

        @pl.when(i == 1)
        def _():
            got(1, ("left", 0))
            send(1, *both("core_right"))
            got(1, ("right", 1))
            send(1, *both("core_left"))
            got(1, *both("core_right"))

        @pl.when(i == 2)
        def _():
            got(1, *both("core_left"))

        @pl.when(i == 3)
        def _():
            got(1, ("pass_right", 0), ("pass_left", 1))
            send(1, *both("core_far"))
            got(1, *both("core_far"))
            start(0)

        gradient(chip_at(i))
        return carry

    lax.fori_loop(0, 4, forwards, 0)
    lax.fori_loop(0, 4, gradients, 0)
    load_g2.start()
    lax.fori_loop(0, 4, widens, 0)
    start(1)
    start(2)
    for a, name, half in sent:
        if a == 0:
            hop(a, name, half).wait_send()
    for b in range(8):
        part = jnp.broadcast_to(racc[:, b * 128 : (b + 1) * 128], (16, 128))
        xg[b // 2, b % 2, 1440:1456, :] = jnp.where(rowid == ex, part, 0.0).astype(BF16)
    load_g2.wait()
    ig_chip(0)
    ig_chip(1)
    advance(0, 0)
    ig_chip(2)
    ig_chip(3)
    sib_copy.start()
    advance(1, 0)
    advance(2, 0)
    ig_pair()
    advance(0, 1)
    ig_step(0)
    advance(0, 2)
    advance(1, 1)
    advance(2, 1)
    ig_step(1)
    advance(0, 3)
    advance(1, 2)
    advance(2, 2)
    ig_step(2)
    advance(1, 3)
    advance(2, 3)
    sib_copy.wait_send()
    for h in range(2):
        for t in range(3):
            x_copy(h, t).wait_send()
    for m in range(3):
        for s in range(4):
            for t in range(3):
                first_copy(m, s, t).wait_send()
                second_copy(m, s, t).wait_send()
    for a, name, half in sent:
        if a == 1:
            hop(a, name, half).wait_send()


def layer(x, og, ids, probs, wg, wu, wd):
    hbm = pl.BlockSpec(memory_space=pl.ANY)
    vmem = pl.BlockSpec(memory_space=pltpu.VMEM)
    return pl.pallas_call(
        kernel,
        out_shape=(
            jax.ShapeDtypeStruct((3, 90, 1, 1440), F32),
            jax.ShapeDtypeStruct((1440, 128), BF16),
            jax.ShapeDtypeStruct((4, 128), BF16),
        ),
        in_specs=[hbm, hbm, vmem, vmem, hbm, hbm, hbm],
        out_specs=(vmem,) * 3,
        scratch_shapes=[
            pltpu.VMEM((4, 2, 1456, 128), BF16),
            pltpu.VMEM((4, 2, 1536, 128), BF16),
            pltpu.VMEM((1536, 1024), BF16),
            pltpu.VMEM((1536, 1024), BF16),
            pltpu.VMEM((2, 1536, 1024), BF16),
            pltpu.VMEM((1440, 1440), BF16),
            pltpu.VMEM((1440, 1440), BF16),
            pltpu.VMEM((3, 4, 768, 768), BF16),
            pltpu.VMEM((3, 4, 3, 192, 768), BF16),
            pltpu.VMEM((3, 4, 3, 48, 768), BF16),
            pltpu.VMEM((4, 1456, 128), BF16),
            pltpu.VMEM((2, 3, 736, 128), BF16),
            pltpu.VMEM((768, 720), BF16),
            pltpu.VMEM((1, 1024), F32),
            pltpu.SemaphoreType.DMA((6,)),
            pltpu.SemaphoreType.DMA((2, 8, 2)),
            pltpu.SemaphoreType.DMA((2, 8, 2)),
            pltpu.SemaphoreType.DMA((3, 4, 6)),
            pltpu.SemaphoreType.DMA((3, 4, 6)),
            pltpu.SemaphoreType.DMA,
            pltpu.SemaphoreType.DMA,
            pltpu.SemaphoreType.DMA((2, 3)),
            pltpu.SemaphoreType.DMA((2, 3)),
        ],
        compiler_params=pltpu.CompilerParams(
            collective_id=0, has_side_effects=True, vmem_limit_bytes=64 * 1024 * 1024
        ),
    )(x, og, ids, probs, wg, wu, wd)


def on_device(tokens, out_grad, expert_ids, probs, w_gate, w_up, w_down):
    out, ig, routed = layer(
        tokens.T, out_grad.T, expert_ids.T, probs.T, w_gate[0], w_up[0], w_down[0]
    )
    down, gate, up = [jnp.transpose(out[m], (1, 0, 2)) for m in range(3)]
    return ig.T, routed.T, gate, up, down


def solution(mesh):
    tok = P(("dp", "expert"), None)
    w = P("expert", None, None)
    g = P("expert", "dp", None)
    return jax.shard_map(
        on_device,
        mesh=mesh,
        in_specs=(tok, tok, tok, tok, w, w, w),
        out_specs=(tok, tok, g, g, g),
        check_vma=False,
    )
```

```python
import functools

import jax
import jax.numpy as jnp
from jax import lax
from jax.experimental import pallas as pl
from jax.experimental.pallas import tpu as pltpu
from jax.sharding import PartitionSpec as P

BF16, F32 = jnp.bfloat16, jnp.float32
MESH = pl.DeviceIdType.MESH
NT = (((1,), (1,)), ((), ()))
NN = (((1,), (0,)), ((), ()))
CHIP = 256


def mod4(v):
    return lax.rem(v + 8, 4)


def place():
    dp = lax.axis_index("dp")
    ex = lax.axis_index("expert")
    return dp // 4, lax.rem(dp, 4), ex // 2, lax.rem(ex, 2)


def kernel(
    x_h, og_h, ids, probs, wg_h, wu_h, wd_h,
    out_h, ig_out, routed,
    xg, og, xp, hp, gu, wa, wb, terms, r1, r2, sib, rx, spread, racc, out,
    load, g_send, g_recv, s_send, s_recv, b_send, b_recv, x_send, x_recv, store,
):
    y, z, x, c = place()
    dp, ex = y * 4 + z, x * 2 + c

    def at(dp_to=None, ex_to=None):
        return (dp if dp_to is None else dp_to, ex if ex_to is None else ex_to)

    def along(axis, d):
        if axis == "y":
            return at(dp_to=mod4(y + d) * 4 + z)
        if axis == "z":
            return at(dp_to=y * 4 + mod4(z + d))
        return at(ex_to=mod4(x + d) * 2 + c)


    own_x = pltpu.make_async_copy(x_h, xg.at[x, c, 0:1440], load.at[0])
    own_og = pltpu.make_async_copy(og_h, og.at[x, c, 0:1440], load.at[1])
    load_g = pltpu.make_async_copy(wg_h, wa, load.at[2])
    load_u = pltpu.make_async_copy(wu_h, wb, load.at[3])
    load_d = pltpu.make_async_copy(wd_h, wa, load.at[4])
    load_g2 = pltpu.make_async_copy(wg_h, wa, load.at[5])
    own_x.start()
    sibling = at(ex_to=x * 2 + 1 - c)
    barrier = pltpu.get_barrier_semaphore()
    for to in [along(a, d) for a in "xyz" for d in (1, -1)] + [sibling]:
        pl.semaphore_signal(barrier, inc=1, device_id=to, device_id_type=MESH)

    left, right, far = mod4(x - 1), mod4(x + 1), mod4(x + 2)

    def hop(a, kind, half, got=False):
        buf = (xg, og)[a]
        rows = slice(0, 768) if half == 0 else slice(768, 1456 if a == 0 else 1440)
        n, sent, arrived, to = {
            "right": (0, x, left, along("x", 1)),
            "left": (1, x, right, along("x", -1)),
            "pass_right": (2, left, far, along("x", 1)),
            "pass_left": (3, right, far, along("x", -1)),
            "core_own": (4, x, x, sibling),
            "core_left": (5, left, left, sibling),
            "core_right": (6, right, right, sibling),
            "core_far": (7, far, far, sibling),
        }[kind]
        core = 1 - c if got and n >= 4 else c
        block = buf.at[arrived if got else sent, core, rows]
        return pltpu.make_async_remote_copy(
            src_ref=block, dst_ref=block, send_sem=g_send.at[a, n, half],
            recv_sem=g_recv.at[a, n, half], device_id=to, device_id_type=MESH,
        )

    sent = []

    def send(a, *names):
        for name, half in names:
            hop(a, name, half).start()
            sent.append((a, name, half))

    def got(a, *names):
        for name, half in names:
            hop(a, name, half, got=True).wait_recv()

    def both(name):
        return (name, 0), (name, 1)

    rowid = lax.broadcasted_iota(jnp.int32, (16, 128), 0)
    dense = jnp.zeros((16, 128), F32)
    for k in range(4):
        dense = dense + jnp.where(ids[k : k + 1, :] == rowid, probs[k : k + 1, :].astype(F32), 0.0)
    xg[x, c, 1440:1456, :] = dense.astype(BF16)
    own_x.wait()
    for copy in (load_g, load_u, own_og):
        copy.start()
    row = lax.broadcasted_iota(jnp.int32, (768, 1), 0)
    rest = row - 384
    above = lax.div(row, 192) * 360 + lax.div(lax.rem(row, 192), 48) * 90 + lax.rem(row, 48)
    below = lax.rem(lax.div(rest, 48), 2) * 360 + lax.div(rest, 96) * 90 + 48 + lax.rem(rest, 48)
    below = jnp.where(lax.rem(row, 48) < 42, below, -1)
    source = jnp.where(row < 384, above, below)
    picked = source == lax.broadcasted_iota(jnp.int32, (768, 720), 1)
    spread[...] = jnp.where(picked, 1.0, 0.0).astype(BF16)
    pl.semaphore_wait(barrier, 7)
    send(0, ("right", 0), ("left", 1), *both("core_own"))

    def flip(w, m):
        for k in range(4):
            n = 384 if k < 3 else 288
            t = w[:, k * 384 : k * 384 + n].T
            for h in range(2):
                r0, r1_ = max(k * 384, h * 720), min(k * 384 + n, h * 720 + 720)
                if r0 < r1_:
                    part = t[r0 - k * 384 : r1_ - k * 384]
                    to = slice(r0 - h * 720, r1_ - h * 720)
                    terms[m, 2 * h, to, :] = part[:, 0:768]
                    terms[m, 2 * h + 1, to, 0:672] = part[:, 768:1440]

    def lanes_of(chip):
        return pl.ds(pl.multiple_of(chip * CHIP, CHIP), CHIP)

    def gate_of(chip):
        parts = []
        for k in range(2):
            rows = xg[chip, k, 1440:1456, :].astype(F32)
            parts.append(jnp.sum(jnp.where(rowid == ex, rows, 0.0), axis=0, keepdims=True))
        return jnp.concatenate(parts, axis=1)

    def place_rows(to, h, v, lanes):
        t = lax.dot_general(spread[...], v, NN, preferred_element_type=F32).astype(BF16)
        to[h * 384 : h * 384 + 384, lanes] = t[0:384]
        for k in range(4):
            r0 = 768 + k * 192 + h * 96
            to[r0 : r0 + 96, lanes] = t[384 + k * 96 : 480 + k * 96]

    def forward(chip):
        lanes = lanes_of(chip)
        gate = gate_of(chip)
        cols = jnp.concatenate([xg[chip, 0, 0:1440, :], xg[chip, 1, 0:1440, :]], axis=1)
        for h in range(2):
            rows = slice(h * 720, h * 720 + 720)
            g, u = [
                lax.dot_general(
                    terms[m, 2 * h, 0:720, :], cols[0:768], NN, preferred_element_type=F32
                )
                + lax.dot_general(
                    terms[m, 2 * h + 1, 0:720, 0:672], cols[768:1440], NN, preferred_element_type=F32
                )
                for m in range(2)
            ]
            s = 0.5 * jnp.tanh(0.5 * g) + 0.5
            gs = g * s
            hidden = gs * u
            gu[0, rows, lanes] = (u * (s + gs * (1.0 - s))).astype(BF16)
            gu[1, rows, lanes] = gs.astype(BF16)
            xp[rows, lanes] = hidden.astype(BF16)
            place_rows(hp, h, (gate * hidden).astype(BF16), lanes)

    def gradient(chip):
        lanes = lanes_of(chip)
        gate = gate_of(chip)
        cols = jnp.concatenate([og[chip, 0, 0:1440, :], og[chip, 1, 0:1440, :]], axis=1)
        total = jnp.zeros((1, CHIP), F32)
        for h in range(2):
            rows = slice(h * 720, h * 720 + 720)
            a = lax.dot_general(wa[rows, :], cols, NN, preferred_element_type=F32)
            pa = gate * a
            gu[0, rows, lanes] = (pa * gu[0, rows, lanes].astype(F32)).astype(BF16)
            gu[1, rows, lanes] = (pa * gu[1, rows, lanes].astype(F32)).astype(BF16)
            hidden = xp[rows, lanes].astype(F32)
            total = total + jnp.sum(hidden * a, axis=0, keepdims=True)
        racc[:, lanes] = total

    def widen(chip):
        for h in range(2):
            rows = slice(h * 720, h * 720 + 720)
            v = jnp.concatenate([xg[chip, 0, rows, :], xg[chip, 1, rows, :]], axis=1)
            place_rows(xp, h, v, lanes_of(chip))

    def way(s):
        first = 1 - s // 2
        d = 1 - 2 * lax.rem(s, 2)
        return first, d

    def step_to(on_y, d):
        return at(dp_to=mod4(y + d * on_y) * 4 + mod4(z + d * (1 - on_y)))

    def chunk(index):
        return pl.ds(pl.multiple_of(index * 192, 64), 192)

    def share(index):
        return pl.ds(pl.multiple_of(index * 48, 16), 48)

    def first_copy(m, s, t):
        on_y, d = way(s)
        pos = y * on_y + z * (1 - on_y)
        go = -d if t == 1 else d
        src = r1.at[m, s, 0] if t == 2 else terms.at[m, s, chunk(mod4(pos + (2 * d, -d)[t]))]
        return pltpu.make_async_remote_copy(
            src_ref=src, dst_ref=r1.at[m, s, t], send_sem=s_send.at[m, s, t],
            recv_sem=s_recv.at[m, s, t], device_id=step_to(on_y, go), device_id_type=MESH,
        )

    def second_copy(m, s, t):
        on_y, d = way(s)
        pos = z * on_y + y * (1 - on_y)
        go = -d if t == 1 else d
        src = r2.at[m, s, 0] if t == 2 else r1.at[m, s, 2, share(mod4(pos + (2 * d, -d)[t]))]
        return pltpu.make_async_remote_copy(
            src_ref=src, dst_ref=r2.at[m, s, t], send_sem=s_send.at[m, s, 3 + t],
            recv_sem=s_recv.at[m, s, 3 + t], device_id=step_to(1 - on_y, go), device_id_type=MESH,
        )

    def start(m):
        def body(s, carry):
            r0 = pl.multiple_of((s // 2) * 768, 768)
            c0 = pl.multiple_of(lax.rem(s, 2) * 768, 768)
            a = (hp if m == 0 else xp)[pl.ds(r0, 768), :]
            if m == 0:
                parts = [og[k // 2, k % 2, pl.ds(c0, 768), :] for k in range(8)]
                b = jnp.concatenate(parts, axis=1)
            else:
                b = gu[m - 1, pl.ds(c0, 768), :]
            terms[m, s] = lax.dot_general(a, b, NT, preferred_element_type=F32).astype(BF16)
            first_copy(m, s, 0).start()
            return carry

        def near(s, carry):
            first_copy(m, s, 1).start()
            return carry

        lax.fori_loop(0, 4, body, 0)
        lax.fori_loop(0, 4, near, 0)

    def stored(m):
        return pltpu.make_async_copy(out.at[m], out_h.at[m], store.at[m])

    def advance(m, stage):
        def body(s, carry):
            on_y, d = way(s)
            if stage < 2:
                pos = y * on_y + z * (1 - on_y)
                if stage == 0:
                    first_copy(m, s, 0).wait_recv()
                    r1[m, s, 0] = r1[m, s, 0] + terms[m, s, chunk(mod4(pos + d)), :]
                    first_copy(m, s, 2).start()
                else:
                    first_copy(m, s, 1).wait_recv()
                    first_copy(m, s, 2).wait_recv()
                    mine = terms[m, s, chunk(pos), :].astype(F32) + r1[m, s, 1].astype(F32)
                    r1[m, s, 2] = (r1[m, s, 2].astype(F32) + mine).astype(BF16)
                    second_copy(m, s, 0).start()
                    second_copy(m, s, 1).start()
                return carry
            pos = z * on_y + y * (1 - on_y)
            if stage == 2:
                second_copy(m, s, 0).wait_recv()
                r2[m, s, 0] = r2[m, s, 0] + r1[m, s, 2, share(mod4(pos + d)), :]
                second_copy(m, s, 2).start()
            else:
                second_copy(m, s, 1).wait_recv()
                second_copy(m, s, 2).wait_recv()
                mine = r1[m, s, 2, share(pos), :].astype(F32)
                total = r2[m, s, 1].astype(F32) + r2[m, s, 2].astype(F32) + mine
                r0, n = 48 * (s // 2), 48 - 6 * (s // 2)
                lanes = (s % 2) * 768
                width = 768 - 96 * (s % 2)
                out[m, r0 : r0 + n, 0, lanes : lanes + width] = total[0:n, 0:width]
            return carry

        if stage < 3:
            lax.fori_loop(0, 4, body, 0)
        else:
            for s in range(4):
                body(s, 0)
            stored(m).start()

    def ig_chip(chip):
        lanes = slice(chip * CHIP, chip * CHIP + CHIP)

        def body(h, carry):
            rows = pl.ds(pl.multiple_of(h * 720, 16), 720)
            t = lax.dot_general(wa[rows, :], gu[0, 0:1440, lanes], NN, preferred_element_type=F32)
            u = lax.dot_general(wb[rows, :], gu[1, 0:1440, lanes], NN, preferred_element_type=F32)
            t = (t + u).astype(BF16)
            xg[chip, 0, rows, :] = t[:, 0:128]
            xg[chip, 1, rows, :] = t[:, 128:256]
            return carry

        lax.fori_loop(0, 2, body, 0)

    sib_copy = pltpu.make_async_remote_copy(
        src_ref=xg.at[:, 1 - c], dst_ref=sib, send_sem=b_send, recv_sem=b_recv,
        device_id=sibling, device_id_type=MESH,
    )
    halves = ((1, 0, 720), (-1, 720, 736))

    def x_copy(h, t):
        d, lo, n = halves[h]
        src = sib.at[mod4(x - d), lo : lo + n] if t == 0 else rx.at[h, t - 1, 0:n]
        return pltpu.make_async_remote_copy(
            src_ref=src, dst_ref=rx.at[h, t, 0:n], send_sem=x_send.at[h, t],
            recv_sem=x_recv.at[h, t], device_id=along("x", d), device_id_type=MESH,
        )

    def ig_pair():
        sib_copy.wait_recv()
        for k in range(4):
            sib[k] = sib[k] + xg[k, c]
        for h in range(2):
            x_copy(h, 0).start()

    def ig_step(t):
        for h in range(2):
            d, lo, n = halves[h]
            x_copy(h, t).wait_recv()
            own = sib[mod4(x - d * (2 + t)), lo : lo + n]
            if t < 2:
                rx[h, t, 0:n] = rx[h, t, 0:n] + own
                x_copy(h, t + 1).start()
            else:
                total = rx[h, t, 0:n].astype(F32) + own.astype(F32)
                ig_out[lo : lo + 720, :] = total[0:720].astype(BF16)
                if h == 1:
                    for k in range(4):
                        mine = jnp.where(ids[k : k + 1, :] == rowid, total[720:736], 0.0)
                        routed[k : k + 1, :] = jnp.sum(mine, axis=0, keepdims=True).astype(BF16)

    load_g.wait()
    flip(wa, 0)
    load_d.start()
    load_u.wait()
    flip(wb, 1)
    hop(0, "right", 0).wait_send()
    sent.remove((0, "right", 0))
    send(0, ("right", 1))
    hop(0, "left", 1).wait_send()
    sent.remove((0, "left", 1))
    send(0, ("left", 0))

    def chip_at(i):
        return mod4(x + i + (i // 2) * (1 - 2 * lax.rem(i, 2)))

    def forwards(i, carry):
        @pl.when(i == 0)
        def _():
            got(0, *both("core_own"))

        @pl.when(i == 1)
        def _():
            got(0, ("right", 0))
            send(0, ("pass_right", 0))
            got(0, ("left", 1))
            send(0, ("pass_left", 1))
            own_og.wait()
            send(1, ("right", 0), ("left", 1), *both("core_own"))
            got(0, ("left", 0))
            send(0, *both("core_right"))
            got(0, ("right", 1))
            send(0, *both("core_left"))
            got(0, *both("core_right"))

        @pl.when(i == 2)
        def _():
            send(1, ("right", 1), ("left", 0))
            got(0, *both("core_left"))

        @pl.when(i == 3)
        def _():
            got(0, ("pass_right", 0), ("pass_left", 1))
            send(0, *both("core_far"))
            got(1, ("right", 0))
            send(1, ("pass_right", 0))
            got(1, ("left", 1))
            send(1, ("pass_left", 1))
            got(0, *both("core_far"))

        forward(chip_at(i))
        return carry

    def widens(i, carry):
        widen(chip_at(i))
        return carry

    def gradients(i, carry):
        @pl.when(i == 0)
        def _():
            load_d.wait()
            got(1, *both("core_own"))

        @pl.when(i == 1)
        def _():
            got(1, ("left", 0))
            send(1, *both("core_right"))
            got(1, ("right", 1))
            send(1, *both("core_left"))
            got(1, *both("core_right"))

        @pl.when(i == 2)
        def _():
            got(1, *both("core_left"))

        @pl.when(i == 3)
        def _():
            got(1, ("pass_right", 0), ("pass_left", 1))
            send(1, *both("core_far"))
            got(1, *both("core_far"))
            start(0)

        gradient(chip_at(i))
        return carry

    lax.fori_loop(0, 4, forwards, 0)
    lax.fori_loop(0, 4, gradients, 0)
    load_g2.start()
    lax.fori_loop(0, 4, widens, 0)
    start(1)
    start(2)
    for a, name, half in sent:
        if a == 0:
            hop(a, name, half).wait_send()
    for b in range(8):
        part = jnp.broadcast_to(racc[:, b * 128 : (b + 1) * 128], (16, 128))
        xg[b // 2, b % 2, 1440:1456, :] = jnp.where(rowid == ex, part, 0.0).astype(BF16)
    load_g2.wait()
    ig_chip(0)
    ig_chip(1)
    advance(0, 0)
    ig_chip(2)
    ig_chip(3)
    sib_copy.start()
    advance(1, 0)
    advance(2, 0)
    ig_pair()
    advance(0, 1)
    ig_step(0)
    advance(0, 2)
    advance(1, 1)
    advance(2, 1)
    ig_step(1)
    advance(0, 3)
    advance(1, 2)
    advance(2, 2)
    ig_step(2)
    advance(1, 3)
    advance(2, 3)
    for m in range(3):
        stored(m).wait()
    sib_copy.wait_send()
    for h in range(2):
        for t in range(3):
            x_copy(h, t).wait_send()
    for m in range(3):
        for s in range(4):
            for t in range(3):
                first_copy(m, s, t).wait_send()
                second_copy(m, s, t).wait_send()
    for a, name, half in sent:
        if a == 1:
            hop(a, name, half).wait_send()


def layer(x, og, ids, probs, wg, wu, wd):
    hbm = pl.BlockSpec(memory_space=pl.ANY)
    vmem = pl.BlockSpec(memory_space=pltpu.VMEM)
    return pl.pallas_call(
        kernel,
        out_shape=(
            jax.ShapeDtypeStruct((3, 90, 1, 1440), F32),
            jax.ShapeDtypeStruct((1440, 128), BF16),
            jax.ShapeDtypeStruct((4, 128), BF16),
        ),
        in_specs=[hbm, hbm, vmem, vmem, hbm, hbm, hbm],
        out_specs=(hbm, vmem, vmem),
        scratch_shapes=[
            pltpu.VMEM((4, 2, 1456, 128), BF16),
            pltpu.VMEM((4, 2, 1536, 128), BF16),
            pltpu.VMEM((1536, 1024), BF16),
            pltpu.VMEM((1536, 1024), BF16),
            pltpu.VMEM((2, 1536, 1024), BF16),
            pltpu.VMEM((1440, 1440), BF16),
            pltpu.VMEM((1440, 1440), BF16),
            pltpu.VMEM((3, 4, 768, 768), BF16),
            pltpu.VMEM((3, 4, 3, 192, 768), BF16),
            pltpu.VMEM((3, 4, 3, 48, 768), BF16),
            pltpu.VMEM((4, 1456, 128), BF16),
            pltpu.VMEM((2, 3, 736, 128), BF16),
            pltpu.VMEM((768, 720), BF16),
            pltpu.VMEM((1, 1024), F32),
            pltpu.VMEM((3, 90, 1, 1440), F32),
            pltpu.SemaphoreType.DMA((6,)),
            pltpu.SemaphoreType.DMA((2, 8, 2)),
            pltpu.SemaphoreType.DMA((2, 8, 2)),
            pltpu.SemaphoreType.DMA((3, 4, 6)),
            pltpu.SemaphoreType.DMA((3, 4, 6)),
            pltpu.SemaphoreType.DMA,
            pltpu.SemaphoreType.DMA,
            pltpu.SemaphoreType.DMA((2, 3)),
            pltpu.SemaphoreType.DMA((2, 3)),
            pltpu.SemaphoreType.DMA((3,)),
        ],
        compiler_params=pltpu.CompilerParams(
            collective_id=0, has_side_effects=True, vmem_limit_bytes=64 * 1024 * 1024
        ),
    )(x, og, ids, probs, wg, wu, wd)


def on_device(tokens, out_grad, expert_ids, probs, w_gate, w_up, w_down):
    out, ig, routed = layer(
        tokens.T, out_grad.T, expert_ids.T, probs.T, w_gate[0], w_up[0], w_down[0]
    )
    down, gate, up = [jnp.transpose(out[m], (1, 0, 2)) for m in range(3)]
    return ig.T, routed.T, gate, up, down


def solution(mesh):
    tok = P(("dp", "expert"), None)
    w = P("expert", None, None)
    g = P("expert", "dp", None)
    return jax.shard_map(
        on_device,
        mesh=mesh,
        in_specs=(tok, tok, tok, tok, w, w, w),
        out_specs=(tok, tok, g, g, g),
        check_vma=False,
    )
```
